512 devices in a mesh: dp: 32 (over x, y, core), tensor: 16 (over z).
Axes of the slice: x: 4, y: 4, z: 16, core: 2. Of those that a mesh axis runs over, the one named last changes fastest.
Arguments:
- stored_rows: bfloat16 [1024, 14336], P(('dp', 'tensor')), may hold values from -6 to 6
- kv_weight: bfloat16 [14336, 2, 14336], P('dp', None, 'tensor'), may hold values from -0.046875 to 0.046875
- lengths: int32 [64], replicated, may hold values from 1 to 16, 768 in all
- new_place: int32 [64], replicated, may hold values from 0 to 63, each once
- query: bfloat16 [64, 14336], P('dp', 'tensor'), may hold values from -80 to 80
- new_kv: bfloat16 [64, 2, 14336], P('dp', None, 'tensor'), may hold values from -4 to 4
Outputs:
- kv_cache: bfloat16 [64, 16, 2, 14336], P('dp', None, None, 'tensor')
- attended: bfloat16 [64, 14336], P('dp', 'tensor')
The draws below stay inside these ranges and needn't reach their ends.
Inputs may be any that keep to these rules, and one draw needn't show every extreme that they name: `new_place`: each request is given a different new slot.
All inputs are finite; a program needn't handle non-finite values.
Results may differ from the reference program's by a relative error of at most 0.035.
Values may be sent and summed in bfloat16 or wider, within the bound.
No kernel may reach another device: no remote copies, remote signals or barrier semaphores. Data moves between devices by JAX's collectives and lax.ppermute only.
A program may use at most 64 MiB of HBM per device.

```python
import math
import jax
import jax.numpy as jnp
import numpy as np
from jax import lax

D = 14336
HEADS = 112
HD = 128
LMAX = 16
REQS = 64
N_DP = 32


def shared_keys(key):
    return jnp.clip(jax.random.normal(key, (REQS, HEADS * HD), jnp.float32), -4.0, 4.0)


def draw_new_kv(key, part):
    base = shared_keys(key)
    key = jax.random.fold_in(key, 11)
    values = jnp.clip(jax.random.normal(key, (REQS, HEADS * HD), jnp.float32), -4.0, 4.0)
    return jnp.stack([base, values], axis=1).astype(jnp.bfloat16)


def draw_query(key, part):
    key = jax.random.fold_in(key, 17)
    first = jax.random.fold_in(key, 0)
    drawn = jnp.clip(jax.random.normal(first, (REQS, HEADS * HD), jnp.float32), -4.0, 4.0)
    return drawn.astype(jnp.bfloat16)


def shard_levels(stream_key, dims, pieces, low, largest):
    level, own = 1.0, jax.random.fold_in(stream_key, 6)
    for axis_at, blocks in pieces:
        draws = jnp.exp(jax.random.uniform(jax.random.fold_in(own, axis_at), (blocks,), jnp.float32, low / len(pieces), largest / len(pieces)))
        level = level * jnp.repeat(draws, dims[axis_at] // blocks).reshape([-1 if axis == axis_at else 1 for axis in range(len(dims))])
    return level


def profile(amount, total, limit, slope):
    loads = [(1 << 20) // math.isqrt(rank ** slope) + 1 for rank in range(2, amount + 1)]
    surplus, given = total - limit - (amount - 1), [1] * (amount - 1)
    while surplus > 0:
        movable = [i for i in range(amount - 1) if given[i] < limit]
        whole, remaining = sum([loads[i] for i in movable]), surplus
        for i in movable:
            extra = min(limit - given[i], max(1, remaining * loads[i] // whole), surplus)
            given[i] = given[i] + extra
            surplus = surplus - extra
    return np.array([limit] + given)


def ragged_sizes(key, amount, total, reach, slope):
    if amount == 2:
        one = jax.random.randint(key, (), max(1, total - reach), min(reach, total - 1) + 1)
        return jnp.stack([one, total - one])
    sizes = jnp.asarray(profile(amount, total, reach, slope), jnp.int32)
    twos = (amount - 1) // 2
    donor, taker = sizes[1:1 + 2 * twos:2], sizes[2:2 + 2 * twos:2]
    margin = jnp.minimum(donor - 1, reach - taker)
    shifted = jax.random.randint(jax.random.fold_in(key, 1), (twos,), 0, 1 << 20) % (margin + 1)
    sizes = sizes.at[1:1 + 2 * twos:2].set(donor - shifted).at[2:2 + 2 * twos:2].set(taker + shifted)
    return sizes[jax.random.permutation(jax.random.fold_in(key, 2), amount)]


def bell_draw(key, extent, width, reach, cuts=(), held_as=jnp.bfloat16):
    drawn = jax.random.normal(key, extent, jnp.float32) * width
    if len(cuts) > 0:
        drawn = shard_levels(key, extent, cuts, -0.22, 0.18) * drawn
    return jnp.clip(drawn, min=-reach, max=reach).astype(held_as)


def setup_inputs(seed: int = 0) -> dict:
    key_of = jax.random.split(jax.random.key(seed), 7)
    return {
        "stored_rows": bell_draw(key_of[0], (REQS * LMAX, D), 1.0, 6.0, ((0, 512),)),
        "kv_weight": bell_draw(key_of[1], (D, 2, HEADS * HD), D ** -0.5, 0.046875, ((0, 32), (2, 16))),
        "lengths": ragged_sizes(key_of[2], REQS, REQS * LMAX * 3 // 4, LMAX, 2).astype(jnp.int32),
        "new_place": jax.random.permutation(key_of[3], REQS).astype(jnp.int32),
        "query": draw_query(jax.random.fold_in(key_of[6], 71), 0),
        "new_kv": draw_new_kv(jax.random.fold_in(key_of[6], 71), 0),
    }


def alibi_slopes(count):
    closest = 2 ** int(math.floor(math.log2(count)))
    counted = jnp.arange(count, dtype=jnp.float32)
    leading = jnp.exp2(-8.0 * (counted + 1.0) / closest)
    trailing = jnp.exp2(-4.0 * (2.0 * (counted - closest) + 1.0) / closest)
    return jnp.where(counted < closest, leading, trailing)

def attend(cache, query, new_kv, slot_len, slopes):
    slots = query.shape[0]
    heads = slopes.shape[0]
    keys = cache[:, :, 0, :].reshape(slots, LMAX, heads, HD).astype(jnp.float32)
    values = cache[:, :, 1, :].reshape(slots, LMAX, heads, HD).astype(jnp.float32)
    asked = query.reshape(slots, heads, HD).astype(jnp.float32)
    own_key = new_kv[:, 0, :].reshape(slots, heads, HD).astype(jnp.float32)
    own_value = new_kv[:, 1, :].reshape(slots, heads, HD).astype(jnp.float32)
    factor = 1.0 / math.sqrt(HD)
    scores = jnp.einsum('shd,sphd->shp', asked, keys) * factor
    place = jnp.arange(LMAX, dtype=jnp.int32)
    distance = (slot_len[:, None] - place[None, :]).astype(jnp.float32)
    scores = scores - slopes[None, :, None] * distance[:, None, :]
    valid = place[None, :] < slot_len[:, None]
    scores = jnp.where(valid[:, None, :], scores, -jnp.inf)
    own = jnp.einsum('shd,shd->sh', asked, own_key) * factor
    top = jnp.maximum(lax.optimization_barrier(jnp.max(scores, axis=2)), own)
    raised = jnp.exp(scores - top[:, :, None])
    own_raised = jnp.exp(own - top)
    total = lax.optimization_barrier(jnp.sum(raised, axis=2)) + own_raised
    weights = (raised / total[:, :, None]).astype(jnp.bfloat16).astype(jnp.float32)
    own_weight = (own_raised / total).astype(jnp.bfloat16).astype(jnp.float32)
    mixed = jnp.einsum('shp,sphd->shd', weights, values)
    mixed = mixed + own_weight[:, :, None] * own_value
    return mixed.reshape(slots, heads * HD).astype(jnp.bfloat16)

def reference(stored_rows, kv_weight, lengths, new_place, query, new_kv):
    requests = lengths.shape[0]
    source = jnp.zeros((requests,), jnp.int32).at[new_place].set(jnp.arange(requests, dtype=jnp.int32))
    slot_len = lengths[source]
    place = jnp.arange(LMAX, dtype=jnp.int32)
    rows = (source[:, None] * LMAX + place[None, :]).reshape(-1)
    live = (place[None, :] < slot_len[:, None]).reshape(-1, 1)
    picked = jnp.where(live, stored_rows[rows], jnp.zeros((), jnp.bfloat16))
    block = D // N_DP
    columns = 2 * HEADS * HD
    flat = kv_weight.reshape(D, columns)

    def add_block(number, total):
        part = lax.dynamic_slice_in_dim(picked, number * block, block, 1)
        weight = lax.dynamic_slice_in_dim(flat, number * block, block, 0)
        term = jnp.dot(part, weight, preferred_element_type=jnp.float32).astype(jnp.bfloat16)
        term = lax.optimization_barrier(term)
        return total + term.astype(jnp.float32)
    summed = lax.fori_loop(0, N_DP, add_block, jnp.zeros((requests * LMAX, columns), jnp.float32))
    kv_cache = summed.astype(jnp.bfloat16).reshape(requests, LMAX, 2, HEADS * HD)
    slopes = alibi_slopes(HEADS)
    attended = attend(kv_cache, query, new_kv, slot_len, slopes)
    return (kv_cache, attended)
```

```python
import math

import jax
import jax.numpy as jnp
from jax import lax
from jax.sharding import PartitionSpec as P

HEADS = 112
HD = 128
REQ_DEV = 2
LMAX = 16
PAIR = 2


def alibi_slopes(count):
    closest = 2 ** int(math.floor(math.log2(count)))
    counted = jnp.arange(count, dtype=jnp.float32)
    leading = jnp.exp2(-8.0 * (counted + 1.0) / closest)
    trailing = jnp.exp2(-4.0 * (2.0 * (counted - closest) + 1.0) / closest)
    return jnp.where(counted < closest, leading, trailing)


def attend(cache, query, new_kv, slot_len, slopes):
    slots = query.shape[0]
    heads = slopes.shape[0]
    keys = cache[:, :, 0, :].reshape(slots, LMAX, heads, HD)
    values = cache[:, :, 1, :].reshape(slots, LMAX, heads, HD)
    asked = query.reshape(slots, heads, HD)
    own_key = new_kv[:, 0, :].reshape(slots, heads, HD)
    own_value = new_kv[:, 1, :].reshape(slots, heads, HD).astype(jnp.float32)
    factor = 1.0 / math.sqrt(HD)
    scores = jnp.einsum("shd,sphd->shp", asked, keys, preferred_element_type=jnp.float32) * factor
    place = jnp.arange(LMAX, dtype=jnp.int32)
    distance = (slot_len[:, None] - place[None, :]).astype(jnp.float32)
    scores = scores - slopes[None, :, None] * distance[:, None, :]
    valid = place[None, :] < slot_len[:, None]
    scores = jnp.where(valid[:, None, :], scores, -jnp.inf)
    own = jnp.einsum("shd,shd->sh", asked, own_key, preferred_element_type=jnp.float32) * factor
    top = jnp.maximum(jnp.max(scores, axis=2), own)
    raised = jnp.exp(scores - top[:, :, None])
    own_raised = jnp.exp(own - top)
    total = jnp.sum(raised, axis=2) + own_raised
    weights = (raised / total[:, :, None]).astype(jnp.bfloat16)
    own_weight = (own_raised / total).astype(jnp.bfloat16).astype(jnp.float32)
    mixed = jnp.einsum("shp,sphd->shd", weights, values, preferred_element_type=jnp.float32)
    mixed = mixed + own_weight[:, :, None] * own_value
    return mixed.reshape(slots, heads * HD).astype(jnp.bfloat16)


def per_device(stored_rows, kv_weight, lengths, new_place, query, new_kv):
    groups = lax.axis_size("dp")
    planes = lax.axis_size("tensor")
    group_index = lax.axis_index("dp")
    tensor_index = lax.axis_index("tensor")
    core = lax.rem(group_index, PAIR)
    chips = groups // PAIR
    width = stored_rows.shape[1]
    block = width // groups
    requests = lengths.shape[0]
    heads_here = kv_weight.shape[2] // HD
    columns = 2 * kv_weight.shape[2]

    by_chip = stored_rows.reshape(PAIR, chips, PAIR, block)
    first = jnp.concatenate([by_chip[0, :, 0], by_chip[0, :, 1]], axis=1)
    second = jnp.concatenate([by_chip[1, :, 1], by_chip[1, :, 0]], axis=1)
    sent = jnp.stack([first, second], axis=1).reshape(groups, PAIR * block)
    mine = lax.all_to_all(sent, "dp", split_axis=0, concat_axis=0, tiled=True)

    flat_weight = kv_weight.reshape(block, columns)
    other_weight = lax.ppermute(flat_weight, "dp", [(i, i ^ 1) for i in range(groups)])
    weight = jnp.concatenate([flat_weight, other_weight], axis=0)

    every = lax.all_gather(mine, "tensor", axis=0, tiled=True)

    slots = jnp.arange(requests, dtype=jnp.int32)
    at_slot = new_place[None, :] == slots[:, None]
    source = jnp.sum(jnp.where(at_slot, slots[None, :], 0), axis=1)
    slot_len = jnp.sum(jnp.where(at_slot, lengths[None, :], 0), axis=1)
    half = LMAX // PAIR
    step = jnp.arange(half, dtype=jnp.int32)
    plane = (source % 2)[:, None] * half + step[None, :]
    row = plane * groups + (source // 2)[:, None]
    live = (PAIR * step + core)[None, :] < slot_len[:, None]
    row = jnp.where(live, row, -1).reshape(-1)
    route = (row[:, None] == jnp.arange(planes * groups, dtype=jnp.int32)[None, :]).astype(jnp.bfloat16)
    picked = jnp.dot(route, every, preferred_element_type=jnp.float32).astype(jnp.bfloat16)
    partial = jnp.dot(picked, weight, preferred_element_type=jnp.float32).astype(jnp.bfloat16)

    arrived = lax.all_to_all(partial, "dp", split_axis=0, concat_axis=0, tiled=True)
    arrived = arrived.reshape(chips, PAIR, REQ_DEV, half, columns)
    summed = jnp.sum(arrived, axis=0, dtype=jnp.float32).astype(jnp.bfloat16)
    kv_cache = summed.transpose(1, 2, 0, 3).reshape(REQ_DEV, LMAX, 2, heads_here * HD)
    here_len = lax.dynamic_slice_in_dim(slot_len, group_index * REQ_DEV, REQ_DEV)
    slopes = lax.dynamic_slice_in_dim(alibi_slopes(HEADS), tensor_index * heads_here, heads_here)
    attended = attend(kv_cache, query, new_kv, here_len, slopes)
    return (kv_cache, attended)


def solution(mesh):
    placed = (
        P(("dp", "tensor"), None),
        P("dp", None, "tensor"),
        P(),
        P(),
        P("dp", "tensor"),
        P("dp", None, "tensor"),
    )
    return jax.shard_map(
        per_device,
        mesh=mesh,
        in_specs=placed,
        out_specs=(P("dp", None, None, "tensor"), P("dp", "tensor")),
        check_vma=False,
    )
```

```python
import math

import jax
import jax.numpy as jnp
from jax import lax
from jax.experimental import pallas as pl
from jax.experimental.pallas import tpu as pltpu
from jax.sharding import PartitionSpec as P

HEADS = 112
HD = 128
REQ_DEV = 2
LMAX = 16
PAIR = 2


def alibi_slopes(count):
    closest = 2 ** int(math.floor(math.log2(count)))
    counted = jnp.arange(count, dtype=jnp.float32)
    leading = jnp.exp2(-8.0 * (counted + 1.0) / closest)
    trailing = jnp.exp2(-4.0 * (2.0 * (counted - closest) + 1.0) / closest)
    return jnp.where(counted < closest, leading, trailing)


def attend(cache, query, new_kv, slot_len, slopes):
    slots = query.shape[0]
    heads = slopes.shape[0]
    keys = cache[:, :, 0, :].reshape(slots, LMAX, heads, HD)
    values = cache[:, :, 1, :].reshape(slots, LMAX, heads, HD)
    asked = query.reshape(slots, heads, HD)
    own_key = new_kv[:, 0, :].reshape(slots, heads, HD)
    own_value = new_kv[:, 1, :].reshape(slots, heads, HD).astype(jnp.float32)
    factor = 1.0 / math.sqrt(HD)
    scores = jnp.einsum("shd,sphd->shp", asked, keys, preferred_element_type=jnp.float32) * factor
    place = jnp.arange(LMAX, dtype=jnp.int32)
    distance = (slot_len[:, None] - place[None, :]).astype(jnp.float32)
    scores = scores - slopes[None, :, None] * distance[:, None, :]
    valid = place[None, :] < slot_len[:, None]
    scores = jnp.where(valid[:, None, :], scores, -jnp.inf)
    own = jnp.einsum("shd,shd->sh", asked, own_key, preferred_element_type=jnp.float32) * factor
    top = jnp.maximum(jnp.max(scores, axis=2), own)
    raised = jnp.exp(scores - top[:, :, None])
    own_raised = jnp.exp(own - top)
    total = jnp.sum(raised, axis=2) + own_raised
    weights = (raised / total[:, :, None]).astype(jnp.bfloat16)
    own_weight = (own_raised / total).astype(jnp.bfloat16).astype(jnp.float32)
    mixed = jnp.einsum("shp,sphd->shd", weights, values, preferred_element_type=jnp.float32)
    mixed = mixed + own_weight[:, :, None] * own_value
    return mixed.reshape(slots, heads * HD).astype(jnp.bfloat16)


def product_kernel(where, x_own, x_other, w_own, w_pair, w_next, w_cross, route, out, xs, ws, rs, sems):
    core, half = where[0], where[1]
    block = w_own.shape[0]

    def rows(at):
        return pl.ds(pl.multiple_of(at * block, 16), block)

    moves = [
        (w_own, ws.at[half, rows(core)]),
        (w_pair, ws.at[half, rows(1 - core)]),
        (w_next, ws.at[1 - half, rows(core)]),
        (w_cross, ws.at[1 - half, rows(1 - core)]),
        (x_own, xs.at[core]),
        (x_other, xs.at[1 - core]),
        (route, rs),
    ]
    copies = [pltpu.make_async_copy(a, b, sems.at[i]) for i, (a, b) in enumerate(moves)]
    for copy in copies:
        copy.start()
    for copy in copies:
        copy.wait()
    columns = out.shape[1]
    for start in range(0, columns, 256):
        part = slice(start, min(start + 256, columns))
        total = jnp.dot(xs[0], ws[0, :, part], preferred_element_type=jnp.float32)
        total += jnp.dot(xs[1], ws[1, :, part], preferred_element_type=jnp.float32)
        placed = jnp.dot(rs[...], total.astype(jnp.bfloat16), preferred_element_type=jnp.float32)
        out[:, part] = placed.astype(jnp.bfloat16)


def product(where, x_own, x_other, w_own, w_pair, w_next, w_cross, route):
    rows, depth = x_own.shape
    block, columns = w_own.shape
    anywhere = pl.BlockSpec(memory_space=pl.ANY)
    return pl.pallas_call(
        product_kernel,
        out_shape=jax.ShapeDtypeStruct((rows, columns), jnp.bfloat16),
        in_specs=[pl.BlockSpec(memory_space=pltpu.SMEM)] + [anywhere] * 7,
        out_specs=pl.BlockSpec(memory_space=pltpu.VMEM),
        scratch_shapes=[
            pltpu.VMEM((2, rows, depth), jnp.bfloat16),
            pltpu.VMEM((2, PAIR * block, columns), jnp.bfloat16),
            pltpu.VMEM(route.shape, jnp.bfloat16),
            pltpu.SemaphoreType.DMA((7,)),
        ],
        compiler_params=pltpu.CompilerParams(vmem_limit_bytes=24 * 1024 * 1024),
        cost_estimate=pl.CostEstimate(
            flops=2 * rows * columns * (2 * depth + rows),
            bytes_accessed=2 * (2 * rows * depth + 4 * block * columns + rows * rows + rows * columns),
            transcendentals=0,
        ),
    )(where, x_own, x_other, w_own, w_pair, w_next, w_cross, route)


def per_device(stored_rows, kv_weight, lengths, new_place, query, new_kv):
    groups = lax.axis_size("dp")
    planes = lax.axis_size("tensor")
    group_index = lax.axis_index("dp")
    tensor_index = lax.axis_index("tensor")
    core = jnp.bitwise_and(group_index, 1)
    half = jnp.bitwise_and(jnp.right_shift(group_index, 3), 1)
    width = stored_rows.shape[1]
    block = width // groups
    requests = lengths.shape[0]
    columns = kv_weight.shape[2]
    heads_here = columns // HD

    sent = stored_rows.reshape(2, 2, 2, 4, 2, block).transpose(1, 0, 3, 2, 4, 5)
    mine = lax.all_to_all(sent.reshape(groups, 2, block), "dp", split_axis=0, concat_axis=0, tiled=True)
    mine = mine.reshape(groups, 2 * block)

    def swapped(array, bit):
        return lax.ppermute(array, "dp", [(i, i ^ bit) for i in range(groups)])

    w_own = lax.dynamic_index_in_dim(kv_weight, core, axis=1, keepdims=False)
    w_away = lax.dynamic_index_in_dim(kv_weight, 1 - core, axis=1, keepdims=False)
    w_next = swapped(w_own, 8)
    w_cross = swapped(w_away, 9)
    w_pair = swapped(w_away, 1)

    slots = jnp.arange(requests, dtype=jnp.int32)
    at_slot = new_place[None, :] == slots[:, None]
    source = jnp.sum(jnp.where(at_slot, slots[None, :], 0), axis=1)
    slot_len = jnp.sum(jnp.where(at_slot, lengths[None, :], 0), axis=1)
    steps = LMAX // 2
    step = jnp.arange(steps, dtype=jnp.int32)
    plane = (source % 2)[:, None] * steps + step[None, :]
    row = plane * groups + (source // 2)[:, None]
    live = (2 * step + half)[None, :] < slot_len[:, None]
    row = jnp.where(live, row, -1).reshape(-1)
    route = (row[:, None] == jnp.arange(planes * groups, dtype=jnp.int32)[None, :]).astype(jnp.bfloat16)

    x_own = lax.all_gather(mine, "tensor", axis=0, tiled=True)
    x_other = swapped(x_own, 1)
    where = jnp.stack([core, half]).astype(jnp.int32)
    partial = product(where, x_own, x_other, w_own, w_pair, w_next, w_cross, route)

    arrived = lax.all_to_all(
        partial.reshape(groups, REQ_DEV * steps, columns), "dp", split_axis=0, concat_axis=0, tiled=True
    )
    arrived = arrived.reshape(2, 2, 4, 2, REQ_DEV, steps, columns)
    summed = jnp.sum(arrived, axis=(0, 2), dtype=jnp.float32).astype(jnp.bfloat16)
    kv_cache = summed.transpose(2, 3, 0, 1, 4).reshape(REQ_DEV, LMAX, 2, columns)
    here_len = lax.dynamic_slice_in_dim(slot_len, group_index * REQ_DEV, REQ_DEV)
    slopes = lax.dynamic_slice_in_dim(alibi_slopes(HEADS), tensor_index * heads_here, heads_here)
    attended = attend(kv_cache, query, new_kv, here_len, slopes)
    return (kv_cache, attended)


def solution(mesh):
    placed = (
        P(("dp", "tensor"), None),
        P("dp", None, "tensor"),
        P(),
        P(),
        P("dp", "tensor"),
        P("dp", None, "tensor"),
    )
    return jax.shard_map(
        per_device,
        mesh=mesh,
        in_specs=placed,
        out_specs=(P("dp", None, None, "tensor"), P("dp", "tensor")),
        check_vma=False,
    )
```

```python
import math

import jax
import jax.numpy as jnp
from jax import lax
from jax.experimental import pallas as pl
from jax.experimental.pallas import tpu as pltpu
from jax.sharding import PartitionSpec as P

HEADS = 112
HD = 128
REQ_DEV = 2
LMAX = 16


def alibi_slopes(count):
    closest = 2 ** int(math.floor(math.log2(count)))
    counted = jnp.arange(count, dtype=jnp.float32)
    leading = jnp.exp2(-8.0 * (counted + 1.0) / closest)
    trailing = jnp.exp2(-4.0 * (2.0 * (counted - closest) + 1.0) / closest)
    return jnp.where(counted < closest, leading, trailing)


def attend(cache, query, new_kv, slot_len, slopes):
    slots = query.shape[0]
    heads = slopes.shape[0]
    keys = cache[:, :, 0, :].reshape(slots, LMAX, heads, HD)
    values = cache[:, :, 1, :].reshape(slots, LMAX, heads, HD)
    asked = query.reshape(slots, heads, HD)
    own_key = new_kv[:, 0, :].reshape(slots, heads, HD)
    own_value = new_kv[:, 1, :].reshape(slots, heads, HD).astype(jnp.float32)
    factor = 1.0 / math.sqrt(HD)
    scores = jnp.einsum("shd,sphd->shp", asked, keys, preferred_element_type=jnp.float32) * factor
    place = jnp.arange(LMAX, dtype=jnp.int32)
    distance = (slot_len[:, None] - place[None, :]).astype(jnp.float32)
    scores = scores - slopes[None, :, None] * distance[:, None, :]
    valid = place[None, :] < slot_len[:, None]
    scores = jnp.where(valid[:, None, :], scores, -jnp.inf)
    own = jnp.einsum("shd,shd->sh", asked, own_key, preferred_element_type=jnp.float32) * factor
    top = jnp.maximum(jnp.max(scores, axis=2), own)
    raised = jnp.exp(scores - top[:, :, None])
    own_raised = jnp.exp(own - top)
    total = jnp.sum(raised, axis=2) + own_raised
    weights = (raised / total[:, :, None]).astype(jnp.bfloat16)
    own_weight = (own_raised / total).astype(jnp.bfloat16).astype(jnp.float32)
    mixed = jnp.einsum("shp,sphd->shd", weights, values, preferred_element_type=jnp.float32)
    mixed = mixed + own_weight[:, :, None] * own_value
    return mixed.reshape(slots, heads * HD).astype(jnp.bfloat16)


def product_kernel(where, x_own, x_other, w_own, w_pair, w_next, w_cross, route, out, xs, ws, rs, sems):
    core, half = where[0], where[1]
    block = w_own.shape[0]
    depth = x_own.shape[1]

    def rows(chip, at):
        return pl.ds(pl.multiple_of(chip * depth + at * block, 16), block)

    def part(at):
        return pl.ds(pl.multiple_of(at * depth, 128), depth)

    moves = [
        (w_next, ws.at[rows(1 - half, core)]),
        (w_cross, ws.at[rows(1 - half, 1 - core)]),
        (w_own, ws.at[rows(half, core)]),
        (w_pair, ws.at[rows(half, 1 - core)]),
        (x_own, xs.at[:, part(core)]),
        (x_other, xs.at[:, part(1 - core)]),
        (route, rs),
    ]
    copies = [pltpu.make_async_copy(a, b, sems.at[i]) for i, (a, b) in enumerate(moves)]
    for copy in copies:
        copy.start()
    for copy in copies:
        copy.wait()
    total = jnp.dot(xs[...], ws[...], preferred_element_type=jnp.float32).astype(jnp.bfloat16)
    out[...] = jnp.dot(rs[...], total, preferred_element_type=jnp.float32).astype(jnp.bfloat16)


def product(where, x_own, x_other, w_own, w_pair, w_next, w_cross, route):
    rows, depth = x_own.shape
    block, columns = w_own.shape
    anywhere = pl.BlockSpec(memory_space=pl.ANY)
    return pl.pallas_call(
        product_kernel,
        out_shape=jax.ShapeDtypeStruct((rows, columns), jnp.bfloat16),
        in_specs=[pl.BlockSpec(memory_space=pltpu.SMEM)] + [anywhere] * 7,
        out_specs=pl.BlockSpec(memory_space=pltpu.VMEM),
        scratch_shapes=[
            pltpu.VMEM((rows, 2 * depth), jnp.bfloat16),
            pltpu.VMEM((4 * block, columns), jnp.bfloat16),
            pltpu.VMEM(route.shape, jnp.bfloat16),
            pltpu.SemaphoreType.DMA((7,)),
        ],
        compiler_params=pltpu.CompilerParams(vmem_limit_bytes=24 * 1024 * 1024),
        cost_estimate=pl.CostEstimate(
            flops=2 * rows * columns * (2 * depth + rows),
            bytes_accessed=2 * (2 * rows * depth + 4 * block * columns + rows * rows + rows * columns),
            transcendentals=0,
        ),
    )(where, x_own, x_other, w_own, w_pair, w_next, w_cross, route)


def per_device(stored_rows, kv_weight, lengths, new_place, query, new_kv):
    groups = lax.axis_size("dp")
    planes = lax.axis_size("tensor")
    group_index = lax.axis_index("dp")
    tensor_index = lax.axis_index("tensor")
    core = jnp.bitwise_and(group_index, 1)
    half = jnp.bitwise_and(jnp.right_shift(group_index, 3), 1)
    width = stored_rows.shape[1]
    block = width // groups
    requests = lengths.shape[0]
    columns = kv_weight.shape[2]
    heads_here = columns // HD

    sent = stored_rows.reshape(2, 2, 2, 4, 2, block).transpose(1, 0, 3, 2, 4, 5)
    mine = lax.all_to_all(sent.reshape(groups, 2, block), "dp", split_axis=0, concat_axis=0, tiled=True)
    mine = mine.reshape(groups, 2 * block)

    def swapped(array, bit):
        return lax.ppermute(array, "dp", [(i, i ^ bit) for i in range(groups)])

    halves = lax.optimization_barrier(kv_weight.transpose(1, 0, 2))
    w_own = lax.dynamic_index_in_dim(halves, core, axis=0, keepdims=False)
    w_away = lax.dynamic_index_in_dim(halves, 1 - core, axis=0, keepdims=False)
    w_next = swapped(w_own, 8)
    w_cross = swapped(w_away, 9)
    w_pair = swapped(w_away, 1)

    slots = jnp.arange(requests, dtype=jnp.int32)
    at_slot = new_place[None, :] == slots[:, None]
    source = jnp.sum(jnp.where(at_slot, slots[None, :], 0), axis=1)
    slot_len = jnp.sum(jnp.where(at_slot, lengths[None, :], 0), axis=1)
    steps = LMAX // 2
    step = jnp.arange(steps, dtype=jnp.int32)
    plane = (source % 2)[:, None] * steps + step[None, :]
    row = plane * groups + (source // 2)[:, None]
    live = (2 * step + half)[None, :] < slot_len[:, None]
    row = jnp.where(live, row, -1).reshape(-1)
    route = (row[:, None] == jnp.arange(planes * groups, dtype=jnp.int32)[None, :]).astype(jnp.bfloat16)

    x_own = lax.all_gather(mine, "tensor", axis=0, tiled=True)
    x_other = swapped(x_own, 1)
    where = jnp.stack([core, half]).astype(jnp.int32)
    partial = product(where, x_own, x_other, w_own, w_pair, w_next, w_cross, route)

    arrived = lax.all_to_all(
        partial.reshape(groups, REQ_DEV * steps, columns), "dp", split_axis=0, concat_axis=0, tiled=True
    )
    arrived = arrived.reshape(2, 2, 4, 2, REQ_DEV, steps, columns)
    summed = jnp.sum(arrived, axis=(0, 2), dtype=jnp.float32).astype(jnp.bfloat16)
    kv_cache = summed.transpose(2, 3, 0, 1, 4).reshape(REQ_DEV, LMAX, 2, columns)
    here_len = lax.dynamic_slice_in_dim(slot_len, group_index * REQ_DEV, REQ_DEV)
    slopes = lax.dynamic_slice_in_dim(alibi_slopes(HEADS), tensor_index * heads_here, heads_here)
    attended = attend(kv_cache, query, new_kv, here_len, slopes)
    return (kv_cache, attended)


def solution(mesh):
    placed = (
        P(("dp", "tensor"), None),
        P("dp", None, "tensor"),
        P(),
        P(),
        P("dp", "tensor"),
        P("dp", None, "tensor"),
    )
    return jax.shard_map(
        per_device,
        mesh=mesh,
        in_specs=placed,
        out_specs=(P("dp", None, None, "tensor"), P("dp", "tensor")),
        check_vma=False,
    )
```

```python
import math

import jax
import jax.numpy as jnp
from jax import lax
from jax.experimental import pallas as pl
from jax.experimental.pallas import tpu as pltpu
from jax.sharding import PartitionSpec as P

HEADS = 112
HD = 128
REQ_DEV = 2
LMAX = 16


def alibi_slopes(count):
    closest = 2 ** int(math.floor(math.log2(count)))
    counted = jnp.arange(count, dtype=jnp.float32)
    leading = jnp.exp2(-8.0 * (counted + 1.0) / closest)
    trailing = jnp.exp2(-4.0 * (2.0 * (counted - closest) + 1.0) / closest)
    return jnp.where(counted < closest, leading, trailing)


def attend(cache, query, new_kv, slot_len, slopes):
    slots = query.shape[0]
    heads = slopes.shape[0]
    keys = cache[:, :, 0, :].reshape(slots, LMAX, heads, HD)
    values = cache[:, :, 1, :].reshape(slots, LMAX, heads, HD)
    asked = query.reshape(slots, heads, HD)
    own_key = new_kv[:, 0, :].reshape(slots, heads, HD)
    own_value = new_kv[:, 1, :].reshape(slots, heads, HD).astype(jnp.float32)
    factor = 1.0 / math.sqrt(HD)
    scores = jnp.einsum("shd,sphd->shp", asked, keys, preferred_element_type=jnp.float32) * factor
    place = jnp.arange(LMAX, dtype=jnp.int32)
    distance = (slot_len[:, None] - place[None, :]).astype(jnp.float32)
    scores = scores - slopes[None, :, None] * distance[:, None, :]
    valid = place[None, :] < slot_len[:, None]
    scores = jnp.where(valid[:, None, :], scores, -jnp.inf)
    own = jnp.einsum("shd,shd->sh", asked, own_key, preferred_element_type=jnp.float32) * factor
    top = jnp.maximum(jnp.max(scores, axis=2), own)
    raised = jnp.exp(scores - top[:, :, None])
    own_raised = jnp.exp(own - top)
    total = jnp.sum(raised, axis=2) + own_raised
    weights = (raised / total[:, :, None]).astype(jnp.bfloat16)
    own_weight = (own_raised / total).astype(jnp.bfloat16).astype(jnp.float32)
    mixed = jnp.einsum("shp,sphd->shd", weights, values, preferred_element_type=jnp.float32)
    mixed = mixed + own_weight[:, :, None] * own_value
    return mixed.reshape(slots, heads * HD).astype(jnp.bfloat16)


VMEM = pl.BlockSpec(memory_space=pltpu.VMEM)
SMEM = pl.BlockSpec(memory_space=pltpu.SMEM)
ANYWHERE = pl.BlockSpec(memory_space=pl.ANY)
KERNEL_VMEM = 24 * 1024 * 1024
SHARE = 2
WIDE, HALF, ROWS_Y, CORES = 2, 2, 4, 2


def split_rows_kernel(rows, sent):
    block = sent.shape[2]
    for wide in range(WIDE):
        for half in range(HALF):
            for y in range(ROWS_Y):
                for core in range(CORES):
                    to = ((wide * HALF + half) * ROWS_Y + y) * CORES + core
                    for part in range(SHARE):
                        chip = half if part == 0 else 1 - half
                        at = ((wide * HALF + chip) * ROWS_Y + y) * CORES + core
                        sent[to, part : part + 1, :] = rows[half : half + 1, at * block : (at + 1) * block]


def split_rows(rows, groups):
    block = rows.shape[1] // groups
    return pl.pallas_call(
        split_rows_kernel,
        out_shape=jax.ShapeDtypeStruct((groups, SHARE, block), jnp.bfloat16),
        in_specs=[VMEM],
        out_specs=VMEM,
        compiler_params=pltpu.CompilerParams(vmem_limit_bytes=KERNEL_VMEM),
    )(rows)


def load_weights(column, w_own, w_next, held, sems):
    block = w_own.shape[1]
    copies = [
        pltpu.make_async_copy(w_own.at[column], held.at[pl.ds(0, block)], sems.at[0]),
        pltpu.make_async_copy(w_next.at[column], held.at[pl.ds(block, block)], sems.at[1]),
    ]
    for copy in copies:
        copy.start()
    return copies


def away_kernel(where, x, w_own, w_next, route, away, picked, held, sems):
    copies = load_weights(1 - where[0], w_own, w_next, held, sems)
    rows = jnp.dot(route[...], x[...], preferred_element_type=jnp.float32).astype(jnp.bfloat16)
    picked[...] = rows
    for copy in copies:
        copy.wait()
    away[...] = jnp.dot(rows, held[...], preferred_element_type=jnp.float32).astype(jnp.bfloat16)


def home_kernel(where, picked, w_own, w_next, home, held, sems):
    for copy in load_weights(where[0], w_own, w_next, held, sems):
        copy.wait()
    home[...] = jnp.dot(picked[...], held[...], preferred_element_type=jnp.float32).astype(jnp.bfloat16)


def product_call(kernel, name, where, x, w_own, w_next, route=()):
    rows, depth = x.shape
    columns = w_own.shape[2]
    one = jax.ShapeDtypeStruct((rows, columns), jnp.bfloat16)
    outs = [one, jax.ShapeDtypeStruct((rows, depth), jnp.bfloat16)] if route else one
    return pl.pallas_call(
        kernel,
        out_shape=outs,
        in_specs=[SMEM, VMEM, ANYWHERE, ANYWHERE] + [VMEM] * len(route),
        out_specs=[VMEM, VMEM] if route else VMEM,
        scratch_shapes=[pltpu.VMEM((depth, columns), jnp.bfloat16), pltpu.SemaphoreType.DMA((2,))],
        compiler_params=pltpu.CompilerParams(vmem_limit_bytes=KERNEL_VMEM),
        cost_estimate=pl.CostEstimate(
            flops=2 * rows * depth * (columns + rows * len(route)),
            bytes_accessed=2 * (rows * depth * (1 + len(route)) + depth * columns + rows * columns),
            transcendentals=0,
        ),
        name=name,
    )(where, x, w_own, w_next, *route)


def per_device(stored_rows, kv_weight, lengths, new_place, query, new_kv):
    groups = lax.axis_size("dp")
    planes = lax.axis_size("tensor")
    group_index = lax.axis_index("dp")
    tensor_index = lax.axis_index("tensor")
    core = jnp.bitwise_and(group_index, 1)
    half = jnp.bitwise_and(jnp.right_shift(group_index, 3), 1)
    width = stored_rows.shape[1]
    block = width // groups
    requests = lengths.shape[0]
    columns = kv_weight.shape[2]
    heads_here = columns // HD

    def swapped(array, bit):
        return lax.ppermute(array, "dp", [(i, i ^ bit) for i in range(groups)])

    mine = lax.all_to_all(split_rows(stored_rows, groups), "dp", split_axis=0, concat_axis=0, tiled=True)
    mine = mine.reshape(groups, SHARE * block)
    w_own = kv_weight.transpose(1, 0, 2)
    w_next = swapped(w_own, ROWS_Y * CORES)

    slots = jnp.arange(requests, dtype=jnp.int32)
    at_slot = new_place[None, :] == slots[:, None]
    source = jnp.sum(jnp.where(at_slot, slots[None, :], 0), axis=1)
    slot_len = jnp.sum(jnp.where(at_slot, lengths[None, :], 0), axis=1)
    steps = LMAX // 2
    step = jnp.arange(steps, dtype=jnp.int32)
    plane = (source % 2)[:, None] * steps + step[None, :]
    row = plane * groups + (source // 2)[:, None]
    live = (2 * step + half)[None, :] < slot_len[:, None]
    row = jnp.where(live, row, -1).reshape(-1)
    route = (row[:, None] == jnp.arange(planes * groups, dtype=jnp.int32)[None, :]).astype(jnp.bfloat16)

    every = lax.all_gather(mine, "tensor", axis=0, tiled=True)
    where = jnp.stack([core, half]).astype(jnp.int32)
    away, picked = product_call(away_kernel, "away", where, every, w_own, w_next, (route,))
    received = swapped(away, 1)
    home = product_call(home_kernel, "home", where, picked, w_own, w_next)
    partial = (home.astype(jnp.float32) + received.astype(jnp.float32)).astype(jnp.bfloat16)

    arrived = lax.all_to_all(
        partial.reshape(groups, REQ_DEV * steps, columns), "dp", split_axis=0, concat_axis=0, tiled=True
    )
    arrived = arrived.reshape(WIDE, HALF, ROWS_Y, CORES, REQ_DEV, steps, columns)
    summed = jnp.sum(arrived, axis=(0, 2), dtype=jnp.float32).astype(jnp.bfloat16)
    kv_cache = summed.transpose(2, 3, 0, 1, 4).reshape(REQ_DEV, LMAX, 2, columns)
    here_len = lax.dynamic_slice_in_dim(slot_len, group_index * REQ_DEV, REQ_DEV)
    slopes = lax.dynamic_slice_in_dim(alibi_slopes(HEADS), tensor_index * heads_here, heads_here)
    attended = attend(kv_cache, query, new_kv, here_len, slopes)
    return (kv_cache, attended)


def solution(mesh):
    placed = (
        P(("dp", "tensor"), None),
        P("dp", None, "tensor"),
        P(),
        P(),
        P("dp", "tensor"),
        P("dp", None, "tensor"),
    )
    return jax.shard_map(
        per_device,
        mesh=mesh,
        in_specs=placed,
        out_specs=(P("dp", None, None, "tensor"), P("dp", "tensor")),
        check_vma=False,
    )
```

```python
import functools
import math

import jax
import jax.numpy as jnp
from jax import lax
from jax.experimental import pallas as pl
from jax.experimental.pallas import tpu as pltpu
from jax.sharding import PartitionSpec as P

HEADS = 112
HD = 128
REQ_DEV = 2
LMAX = 16


def alibi_slopes(count):
    closest = 2 ** int(math.floor(math.log2(count)))
    counted = jnp.arange(count, dtype=jnp.float32)
    leading = jnp.exp2(-8.0 * (counted + 1.0) / closest)
    trailing = jnp.exp2(-4.0 * (2.0 * (counted - closest) + 1.0) / closest)
    return jnp.where(counted < closest, leading, trailing)


def attend(cache, query, new_kv, slot_len, slopes):
    slots = query.shape[0]
    heads = slopes.shape[0]
    keys = cache[:, :, 0, :].reshape(slots, LMAX, heads, HD)
    values = cache[:, :, 1, :].reshape(slots, LMAX, heads, HD)
    asked = query.reshape(slots, heads, HD)
    own_key = new_kv[:, 0, :].reshape(slots, heads, HD)
    own_value = new_kv[:, 1, :].reshape(slots, heads, HD).astype(jnp.float32)
    factor = 1.0 / math.sqrt(HD)
    scores = jnp.einsum("shd,sphd->shp", asked, keys, preferred_element_type=jnp.float32) * factor
    place = jnp.arange(LMAX, dtype=jnp.int32)
    distance = (slot_len[:, None] - place[None, :]).astype(jnp.float32)
    scores = scores - slopes[None, :, None] * distance[:, None, :]
    valid = place[None, :] < slot_len[:, None]
    scores = jnp.where(valid[:, None, :], scores, -jnp.inf)
    own = jnp.einsum("shd,shd->sh", asked, own_key, preferred_element_type=jnp.float32) * factor
    top = jnp.maximum(jnp.max(scores, axis=2), own)
    raised = jnp.exp(scores - top[:, :, None])
    own_raised = jnp.exp(own - top)
    total = jnp.sum(raised, axis=2) + own_raised
    weights = (raised / total[:, :, None]).astype(jnp.bfloat16)
    own_weight = (own_raised / total).astype(jnp.bfloat16).astype(jnp.float32)
    mixed = jnp.einsum("shp,sphd->shd", weights, values, preferred_element_type=jnp.float32)
    mixed = mixed + own_weight[:, :, None] * own_value
    return mixed.reshape(slots, heads * HD).astype(jnp.bfloat16)


VMEM = pl.BlockSpec(memory_space=pltpu.VMEM)
SMEM = pl.BlockSpec(memory_space=pltpu.SMEM)
ANYWHERE = pl.BlockSpec(memory_space=pl.ANY)
HBM = pl.BlockSpec(memory_space=pltpu.HBM)
KERNEL_VMEM = 24 * 1024 * 1024
TILE = 512
SIDE = 4
CORES = 2


def partner(index):
    return index ^ (2 * SIDE if index % CORES == 0 else CORES)


def parity(index):
    return (index // (CORES * SIDE) + index // CORES) % 2


def split_rows_kernel(rows, sent):
    groups, share, block = sent.shape
    for to in range(groups):
        row = parity(to)
        for part, at in enumerate((to, partner(to))):
            sent[to, part : part + 1, :] = rows[row : row + 1, at * block : (at + 1) * block]


def split_rows(rows, groups):
    block = rows.shape[1] // groups
    return pl.pallas_call(
        split_rows_kernel,
        out_shape=jax.ShapeDtypeStruct((groups, 2, block), jnp.bfloat16),
        in_specs=[VMEM],
        out_specs=VMEM,
        compiler_params=pltpu.CompilerParams(vmem_limit_bytes=KERNEL_VMEM),
        name="split_rows",
    )(rows)


def join_rows_kernel(parts, rows):
    block = parts.shape[2]
    rows[:, :block] = parts[:, 0, :]
    rows[:, block:] = parts[:, 1, :]


def join_rows(parts):
    groups, share, block = parts.shape
    return pl.pallas_call(
        join_rows_kernel,
        out_shape=jax.ShapeDtypeStruct((groups, share * block), jnp.bfloat16),
        in_specs=[VMEM],
        out_specs=VMEM,
        compiler_params=pltpu.CompilerParams(vmem_limit_bytes=KERNEL_VMEM),
        cost_estimate=pl.CostEstimate(flops=34500000000, bytes_accessed=0, transcendentals=0),
        name="join_rows",
    )(parts)


def fetch(moves, sems):
    copies = [pltpu.make_async_copy(source, to, sems.at[at]) for at, (source, to) in enumerate(moves)]
    for copy in copies:
        copy.start()
    return copies


def finish(copies):
    for copy in copies:
        copy.wait()


def product_kernel(home, where, x, w_own, w_next, route, out, xs, rs, held, made, sems):
    column = where[0] if home else 1 - where[0]
    block = w_own.shape[1]
    copies = fetch(
        [
            (x, xs),
            (route, rs),
            (w_own.at[column], held.at[pl.ds(0, block)]),
            (w_next.at[column], held.at[pl.ds(block, block)]),
        ],
        sems,
    )
    finish(copies[:2])
    rows = jnp.dot(rs[...], xs[...], preferred_element_type=jnp.float32).astype(jnp.bfloat16)
    finish(copies[2:])
    stores = []
    for at, start in enumerate(range(0, out.shape[1], TILE)):
        part = pl.ds(start, min(TILE, out.shape[1] - start))
        made[:, part] = jnp.dot(rows, held[:, part], preferred_element_type=jnp.float32).astype(jnp.bfloat16)
        stores += fetch([(made.at[:, part], out.at[:, part])], sems.at[pl.ds(4 + at, 1)])
    finish(stores)


def product(home, where, x, w_own, w_next, route):
    rows, depth = x.shape
    columns = w_own.shape[2]
    return pl.pallas_call(
        functools.partial(product_kernel, home),
        out_shape=jax.ShapeDtypeStruct((rows, columns), jnp.bfloat16),
        in_specs=[SMEM, ANYWHERE, ANYWHERE, ANYWHERE, HBM],
        out_specs=ANYWHERE,
        scratch_shapes=[
            pltpu.VMEM(x.shape, jnp.bfloat16),
            pltpu.VMEM(route.shape, jnp.bfloat16),
            pltpu.VMEM((depth, columns), jnp.bfloat16),
            pltpu.VMEM((rows, columns), jnp.bfloat16),
            pltpu.SemaphoreType.DMA((4 + pl.cdiv(columns, TILE),)),
        ],
        compiler_params=pltpu.CompilerParams(vmem_limit_bytes=KERNEL_VMEM),
        cost_estimate=pl.CostEstimate(
            flops=2 * rows * depth * (columns + rows),
            bytes_accessed=2 * (rows * depth + rows * rows + depth * columns + rows * columns),
            transcendentals=0,
        ),
        name="home" if home else "away",
    )(where, x, w_own, w_next, route)


def add_kernel(one, other, total, left, right, sems):
    finish(fetch([(one, left), (other, right)], sems))
    left[...] = (left[...].astype(jnp.float32) + right[...].astype(jnp.float32)).astype(jnp.bfloat16)
    finish(fetch([(left, total)], sems))


def add(one, other):
    return pl.pallas_call(
        add_kernel,
        out_shape=jax.ShapeDtypeStruct(one.shape, jnp.bfloat16),
        in_specs=[ANYWHERE, ANYWHERE],
        out_specs=ANYWHERE,
        scratch_shapes=[pltpu.VMEM(one.shape, jnp.bfloat16)] * 2 + [pltpu.SemaphoreType.DMA((2,))],
        compiler_params=pltpu.CompilerParams(vmem_limit_bytes=KERNEL_VMEM),
        cost_estimate=pl.CostEstimate(flops=one.size, bytes_accessed=6 * one.size, transcendentals=0),
        name="add",
    )(one, other)


def per_device(stored_rows, kv_weight, lengths, new_place, query, new_kv):
    groups = lax.axis_size("dp")
    planes = lax.axis_size("tensor")
    group_index = lax.axis_index("dp")
    tensor_index = lax.axis_index("tensor")
    core = jnp.bitwise_and(group_index, 1)
    half = jnp.bitwise_and(jnp.right_shift(group_index, 3) + jnp.right_shift(group_index, 1), 1)
    requests = lengths.shape[0]
    columns = kv_weight.shape[2]
    heads_here = columns // HD

    sent = split_rows(stored_rows, groups)
    mine = join_rows(lax.all_to_all(sent, "dp", split_axis=0, concat_axis=0, tiled=True))
    w_own = kv_weight.transpose(1, 0, 2)
    w_next = lax.ppermute(w_own, "dp", [(i, partner(i)) for i in range(groups)])

    slots = jnp.arange(requests, dtype=jnp.int32)
    at_slot = new_place[None, :] == slots[:, None]
    source = jnp.sum(jnp.where(at_slot, slots[None, :], 0), axis=1)
    slot_len = jnp.sum(jnp.where(at_slot, lengths[None, :], 0), axis=1)
    steps = LMAX // 2
    step = jnp.arange(steps, dtype=jnp.int32)
    plane = (source % 2)[:, None] * steps + step[None, :]
    row = plane * groups + (source // 2)[:, None]
    live = (2 * step + half)[None, :] < slot_len[:, None]
    row = jnp.where(live, row, -1).reshape(-1)
    route = (row[:, None] == jnp.arange(planes * groups, dtype=jnp.int32)[None, :]).astype(jnp.bfloat16)

    every = lax.all_gather(mine, "tensor", axis=0, tiled=True)
    where = jnp.stack([core, half]).astype(jnp.int32)
    away = product(False, where, every, w_own, w_next, route)
    received = lax.ppermute(away, "dp", [(i, i ^ 1) for i in range(groups)])
    partial = add(product(True, where, every, w_own, w_next, route), received)

    arrived = lax.all_to_all(
        partial.reshape(groups, REQ_DEV * steps, columns), "dp", split_axis=0, concat_axis=0, tiled=True
    )
    arrived = arrived.reshape(2, 2, 2, 2, CORES, REQ_DEV, steps, columns)
    summed = jnp.sum(arrived, axis=(0, 2), dtype=jnp.float32)
    summed = jnp.stack([summed[0, 0] + summed[1, 1], summed[0, 1] + summed[1, 0]]).astype(jnp.bfloat16)
    kv_cache = summed.transpose(2, 3, 0, 1, 4).reshape(REQ_DEV, LMAX, 2, columns)
    here_len = lax.dynamic_slice_in_dim(slot_len, group_index * REQ_DEV, REQ_DEV)
    slopes = lax.dynamic_slice_in_dim(alibi_slopes(HEADS), tensor_index * heads_here, heads_here)
    attended = attend(kv_cache, query, new_kv, here_len, slopes)
    return (kv_cache, attended)


def solution(mesh):
    placed = (
        P(("dp", "tensor"), None),
        P("dp", None, "tensor"),
        P(),
        P(),
        P("dp", "tensor"),
        P("dp", None, "tensor"),
    )
    return jax.shard_map(
        per_device,
        mesh=mesh,
        in_specs=placed,
        out_specs=(P("dp", None, None, "tensor"), P("dp", "tensor")),
        check_vma=False,
    )
```

```python
import functools
import math

import jax
import jax.numpy as jnp
from jax import lax
from jax.experimental import pallas as pl
from jax.experimental.pallas import tpu as pltpu
from jax.sharding import PartitionSpec as P

HEADS = 112
HD = 128
REQ_DEV = 2
LMAX = 16


def alibi_slopes(count):
    closest = 2 ** int(math.floor(math.log2(count)))
    counted = jnp.arange(count, dtype=jnp.float32)
    leading = jnp.exp2(-8.0 * (counted + 1.0) / closest)
    trailing = jnp.exp2(-4.0 * (2.0 * (counted - closest) + 1.0) / closest)
    return jnp.where(counted < closest, leading, trailing)


VMEM = pl.BlockSpec(memory_space=pltpu.VMEM)
SMEM = pl.BlockSpec(memory_space=pltpu.SMEM)
ANYWHERE = pl.BlockSpec(memory_space=pl.ANY)
HBM = pl.BlockSpec(memory_space=pltpu.HBM)
KERNEL_VMEM = 24 * 1024 * 1024
SIDE = 4
CORES = 2


def partner(index):
    return index ^ (2 * SIDE if index % CORES == 0 else CORES)


def parity(index):
    return (index // (CORES * SIDE) + index // CORES) % 2


def split_rows_kernel(rows, sent):
    groups, share, block = sent.shape
    for to in range(groups):
        row = parity(to)
        for part, at in enumerate((to, partner(to))):
            sent[to, part : part + 1, :] = rows[row : row + 1, at * block : (at + 1) * block]


def split_rows(rows, groups):
    block = rows.shape[1] // groups
    return pl.pallas_call(
        split_rows_kernel,
        out_shape=jax.ShapeDtypeStruct((groups, 2, block), jnp.bfloat16),
        in_specs=[VMEM],
        out_specs=VMEM,
        compiler_params=pltpu.CompilerParams(vmem_limit_bytes=KERNEL_VMEM),
        name="split_rows",
    )(rows)


def join_rows_kernel(parts, rows):
    block = parts.shape[2]
    rows[:, :block] = parts[:, 0, :]
    rows[:, block:] = parts[:, 1, :]


def join_rows(parts):
    groups, share, block = parts.shape
    return pl.pallas_call(
        join_rows_kernel,
        out_shape=jax.ShapeDtypeStruct((groups, share * block), jnp.bfloat16),
        in_specs=[VMEM],
        out_specs=VMEM,
        compiler_params=pltpu.CompilerParams(vmem_limit_bytes=KERNEL_VMEM),
        cost_estimate=pl.CostEstimate(flops=34500000000, bytes_accessed=0, transcendentals=0),
        name="join_rows",
    )(parts)


def fetch(moves, sems):
    copies = [pltpu.make_async_copy(source, to, sems.at[at]) for at, (source, to) in enumerate(moves)]
    for copy in copies:
        copy.start()
    return copies


def finish(copies):
    for copy in copies:
        copy.wait()


def product_kernel(home, where, x, w_own, w_next, out):
    column = where[0] if home else 1 - where[0]
    block = w_own.shape[1]
    total = jnp.dot(x[:, :block], w_own[column], preferred_element_type=jnp.float32)
    total += jnp.dot(x[:, block:], w_next[column], preferred_element_type=jnp.float32)
    out[...] = total.astype(jnp.bfloat16)


def product(home, where, x, w_own, w_next):
    rows, depth = x.shape
    columns = w_own.shape[2]
    return pl.pallas_call(
        functools.partial(product_kernel, home),
        out_shape=jax.ShapeDtypeStruct((rows, columns), jnp.bfloat16),
        in_specs=[SMEM, VMEM, VMEM, VMEM],
        out_specs=VMEM,
        compiler_params=pltpu.CompilerParams(vmem_limit_bytes=KERNEL_VMEM),
        cost_estimate=pl.CostEstimate(
            flops=2 * rows * depth * columns,
            bytes_accessed=2 * (rows * depth + depth * columns + rows * columns),
            transcendentals=0,
        ),
        name="home" if home else "away",
    )(where, x, w_own, w_next)


def add_kernel(one, other, route, total, rs, made, sems):
    finish(fetch([(route, rs)], sems))
    both = (one[...].astype(jnp.float32) + other[...].astype(jnp.float32)).astype(jnp.bfloat16)
    made[...] = jnp.dot(rs[...], both, preferred_element_type=jnp.float32).astype(jnp.bfloat16)
    finish(fetch([(made, total)], sems.at[pl.ds(1, 1)]))


def add(one, other, route):
    return pl.pallas_call(
        add_kernel,
        out_shape=jax.ShapeDtypeStruct(one.shape, jnp.bfloat16),
        in_specs=[VMEM, VMEM, HBM],
        out_specs=ANYWHERE,
        scratch_shapes=[
            pltpu.VMEM(route.shape, jnp.bfloat16),
            pltpu.VMEM(one.shape, jnp.bfloat16),
            pltpu.SemaphoreType.DMA((2,)),
        ],
        compiler_params=pltpu.CompilerParams(vmem_limit_bytes=KERNEL_VMEM),
        cost_estimate=pl.CostEstimate(
            flops=2 * one.size * route.shape[0], bytes_accessed=6 * one.size + 2 * route.size, transcendentals=0
        ),
        name="add",
    )(one, other, route)


def attend_kernel(lens, slopes, cache, query, new_kv, result, out):
    del result
    slots, columns = query.shape
    heads = columns // HD
    steps = cache.shape[3]
    factor = 1.0 / math.sqrt(HD)
    head_lane = lax.broadcasted_iota(jnp.int32, (steps, HD), 1)
    slope = jnp.zeros((steps, HD), jnp.float32)
    for head in range(heads):
        slope = jnp.where(head_lane == head, slopes[head], slope)
    for slot in range(slots):
        asked = query[slot : slot + 1, :].astype(jnp.float32)
        own_value = new_kv[slot, 1:2, :].astype(jnp.float32)

        def by_head(rows):
            products = rows * asked
            scores = jnp.zeros((rows.shape[0], HD), jnp.float32)
            for head in range(heads):
                total = jnp.sum(products[:, head * HD : (head + 1) * HD], axis=1, keepdims=True)
                scores = jnp.where(head_lane[: rows.shape[0]] == head, total, scores)
            return scores * factor

        own = by_head(new_kv[slot, 0:1, :].astype(jnp.float32))
        scores = []
        for half in range(2):
            place = 2 * lax.broadcasted_iota(jnp.int32, (steps, HD), 0) + half
            distance = (lens[slot] - place).astype(jnp.float32)
            found = by_head(cache[half, 0, slot].astype(jnp.float32)) - slope * distance
            scores.append(jnp.where(place < lens[slot], found, -jnp.inf))
        top = jnp.maximum(jnp.max(jnp.maximum(scores[0], scores[1]), axis=0, keepdims=True), own)
        raised = [jnp.exp(score - top) for score in scores]
        own_raised = jnp.exp(own - top)
        total = jnp.sum(raised[0] + raised[1], axis=0, keepdims=True) + own_raised
        weights = [(part / total).astype(jnp.bfloat16).astype(jnp.float32) for part in raised]
        own_weight = (own_raised / total).astype(jnp.bfloat16).astype(jnp.float32)
        for head in range(heads):
            lanes = slice(head * HD, (head + 1) * HD)
            mixed = jnp.zeros((steps, HD), jnp.float32)
            for half in range(2):
                values = cache[half, 1, slot, :, lanes].astype(jnp.float32)
                mixed += weights[half][:, head : head + 1] * values
            mixed = jnp.sum(mixed, axis=0, keepdims=True) + own_weight[:, head : head + 1] * own_value[:, lanes]
            out[slot : slot + 1, lanes] = mixed.astype(jnp.bfloat16)


def attend(lens, slopes, cache, query, new_kv, result):
    return pl.pallas_call(
        attend_kernel,
        out_shape=jax.ShapeDtypeStruct(query.shape, jnp.bfloat16),
        in_specs=[SMEM, SMEM, VMEM, VMEM, VMEM, VMEM],
        out_specs=VMEM,
        compiler_params=pltpu.CompilerParams(vmem_limit_bytes=KERNEL_VMEM),
        cost_estimate=pl.CostEstimate(flops=8 * cache.size, bytes_accessed=2 * cache.size, transcendentals=cache.size // HD),
        name="attend",
    )(lens, slopes, cache, query, new_kv, result)


def per_device(stored_rows, kv_weight, lengths, new_place, query, new_kv):
    groups = lax.axis_size("dp")
    planes = lax.axis_size("tensor")
    group_index = lax.axis_index("dp")
    tensor_index = lax.axis_index("tensor")
    core = jnp.bitwise_and(group_index, 1)
    half = jnp.bitwise_and(jnp.right_shift(group_index, 3) + jnp.right_shift(group_index, 1), 1)
    requests = lengths.shape[0]
    columns = kv_weight.shape[2]
    heads_here = columns // HD

    sent = split_rows(stored_rows, groups)
    mine = join_rows(lax.all_to_all(sent, "dp", split_axis=0, concat_axis=0, tiled=True))
    w_own = kv_weight.transpose(1, 0, 2)
    w_next = lax.ppermute(w_own, "dp", [(i, partner(i)) for i in range(groups)])

    slots = jnp.arange(requests, dtype=jnp.int32)
    at_slot = new_place[None, :] == slots[:, None]
    source = jnp.sum(jnp.where(at_slot, slots[None, :], 0), axis=1)
    slot_len = jnp.sum(jnp.where(at_slot, lengths[None, :], 0), axis=1)
    steps = LMAX // 2
    step = jnp.arange(steps, dtype=jnp.int32)
    plane = (source % 2)[:, None] * steps + step[None, :]
    row = plane * groups + (source // 2)[:, None]
    live = (2 * step + half)[None, :] < slot_len[:, None]
    row = jnp.where(live, row, -1).reshape(-1)
    route = (row[:, None] == jnp.arange(planes * groups, dtype=jnp.int32)[None, :]).astype(jnp.bfloat16)

    every = lax.all_gather(mine, "tensor", axis=0, tiled=True)
    where = core.reshape(1).astype(jnp.int32)
    away = product(False, where, every, w_own, w_next)
    received = lax.ppermute(away, "dp", [(i, i ^ 1) for i in range(groups)])
    partial = add(product(True, where, every, w_own, w_next), received, route)

    arrived = lax.all_to_all(
        partial.reshape(groups, REQ_DEV * steps, columns), "dp", split_axis=0, concat_axis=0, tiled=True
    )
    arrived = arrived.reshape(2, 2, 2, 2, CORES, REQ_DEV, steps, columns)
    summed = jnp.sum(arrived, axis=(0, 2), dtype=jnp.float32)
    summed = jnp.stack([summed[0, 0] + summed[1, 1], summed[0, 1] + summed[1, 0]]).astype(jnp.bfloat16)
    kv_cache = summed.transpose(2, 3, 0, 1, 4).reshape(REQ_DEV, LMAX, 2, columns)
    here_len = lax.dynamic_slice_in_dim(slot_len, group_index * REQ_DEV, REQ_DEV)
    slopes = lax.dynamic_slice_in_dim(alibi_slopes(HEADS), tensor_index * heads_here, heads_here)
    return (kv_cache, attend(here_len, slopes, summed, query, new_kv, kv_cache))


def solution(mesh):
    placed = (
        P(("dp", "tensor"), None),
        P("dp", None, "tensor"),
        P(),
        P(),
        P("dp", "tensor"),
        P("dp", None, "tensor"),
    )
    return jax.shard_map(
        per_device,
        mesh=mesh,
        in_specs=placed,
        out_specs=(P("dp", None, None, "tensor"), P("dp", "tensor")),
        check_vma=False,
    )
```

```python
import functools
import math

import jax
import jax.numpy as jnp
from jax import lax
from jax.experimental import pallas as pl
from jax.experimental.pallas import tpu as pltpu
from jax.sharding import PartitionSpec as P

HEADS = 112
HD = 128
REQ_DEV = 2
LMAX = 16


def alibi_slopes(count):
    closest = 2 ** int(math.floor(math.log2(count)))
    counted = jnp.arange(count, dtype=jnp.float32)
    leading = jnp.exp2(-8.0 * (counted + 1.0) / closest)
    trailing = jnp.exp2(-4.0 * (2.0 * (counted - closest) + 1.0) / closest)
    return jnp.where(counted < closest, leading, trailing)


VMEM = pl.BlockSpec(memory_space=pltpu.VMEM)
SMEM = pl.BlockSpec(memory_space=pltpu.SMEM)
ANYWHERE = pl.BlockSpec(memory_space=pl.ANY)
HBM = pl.BlockSpec(memory_space=pltpu.HBM)
KERNEL_VMEM = 24 * 1024 * 1024
SIDE = 4
CORES = 2


def partner(index):
    return index ^ (2 * SIDE if index % CORES == 0 else CORES)


def parity(index):
    return (index // (CORES * SIDE) + index // CORES) % 2


def split_rows_kernel(rows, sent):
    groups, share, block = sent.shape
    for to in range(groups):
        row = parity(to)
        for part, at in enumerate((to, partner(to))):
            sent[to, part : part + 1, :] = rows[row : row + 1, at * block : (at + 1) * block]


def split_rows(rows, groups):
    block = rows.shape[1] // groups
    return pl.pallas_call(
        split_rows_kernel,
        out_shape=jax.ShapeDtypeStruct((groups, 2, block), jnp.bfloat16),
        in_specs=[VMEM],
        out_specs=VMEM,
        compiler_params=pltpu.CompilerParams(vmem_limit_bytes=KERNEL_VMEM),
        name="split_rows",
    )(rows)


def join_rows_kernel(parts, row, rows):
    del row
    block = parts.shape[2]
    rows[:, :block] = parts[:, 0, :]
    rows[:, block:] = parts[:, 1, :]


def join_rows(parts, row):
    groups, share, block = parts.shape
    return pl.pallas_call(
        join_rows_kernel,
        out_shape=jax.ShapeDtypeStruct((groups, share * block), jnp.bfloat16),
        in_specs=[VMEM, HBM],
        out_specs=VMEM,
        compiler_params=pltpu.CompilerParams(vmem_limit_bytes=KERNEL_VMEM),
        cost_estimate=pl.CostEstimate(flops=34500000000, bytes_accessed=0, transcendentals=0),
        name="join_rows",
    )(parts, row)


def fetch(moves, sems):
    copies = [pltpu.make_async_copy(source, to, sems.at[at]) for at, (source, to) in enumerate(moves)]
    for copy in copies:
        copy.start()
    return copies


def finish(copies):
    for copy in copies:
        copy.wait()


def product_kernel(home, where, x, w_own, w_next, out, held, sems):
    column = where[0] if home else 1 - where[0]
    block = w_own.shape[1]
    copies = fetch([(w_next.at[column], held)], sems)
    total = jnp.dot(x[:, :block], w_own[column], preferred_element_type=jnp.float32)
    finish(copies)
    total += jnp.dot(x[:, block:], held[...], preferred_element_type=jnp.float32)
    out[...] = total.astype(jnp.bfloat16)


def product(home, where, x, w_own, w_next):
    rows, depth = x.shape
    columns = w_own.shape[2]
    return pl.pallas_call(
        functools.partial(product_kernel, home),
        out_shape=jax.ShapeDtypeStruct((rows, columns), jnp.bfloat16),
        in_specs=[SMEM, VMEM, VMEM, ANYWHERE],
        out_specs=VMEM,
        scratch_shapes=[pltpu.VMEM(w_next.shape[1:], jnp.bfloat16), pltpu.SemaphoreType.DMA((1,))],
        compiler_params=pltpu.CompilerParams(vmem_limit_bytes=KERNEL_VMEM),
        cost_estimate=pl.CostEstimate(
            flops=2 * rows * depth * columns,
            bytes_accessed=2 * (rows * depth + depth * columns + rows * columns),
            transcendentals=0,
        ),
        name="home" if home else "away",
    )(where, x, w_own, w_next)


def add_kernel(one, other, route, total):
    both = (one[...].astype(jnp.float32) + other[...].astype(jnp.float32)).astype(jnp.bfloat16)
    total[...] = jnp.dot(route[...], both, preferred_element_type=jnp.float32).astype(jnp.bfloat16)


def add(one, other, route):
    return pl.pallas_call(
        add_kernel,
        out_shape=jax.ShapeDtypeStruct(one.shape, jnp.bfloat16),
        in_specs=[VMEM, VMEM, VMEM],
        out_specs=VMEM,
        compiler_params=pltpu.CompilerParams(vmem_limit_bytes=KERNEL_VMEM),
        cost_estimate=pl.CostEstimate(
            flops=2 * one.size * route.shape[0], bytes_accessed=6 * one.size + 2 * route.size, transcendentals=0
        ),
        name="add",
    )(one, other, route)


def attend_kernel(lens, slopes, cache, query, new_kv, result, out):
    del result
    slots, columns = query.shape
    heads = columns // HD
    steps = cache.shape[3]
    factor = 1.0 / math.sqrt(HD)
    head_lane = lax.broadcasted_iota(jnp.int32, (steps, HD), 1)
    slope = jnp.zeros((steps, HD), jnp.float32)
    for head in range(heads):
        slope = jnp.where(head_lane == head, slopes[head], slope)
    for slot in range(slots):
        asked = query[slot : slot + 1, :].astype(jnp.float32)
        own_value = new_kv[slot, 1:2, :].astype(jnp.float32)

        def by_head(rows):
            products = rows * asked
            scores = jnp.zeros((rows.shape[0], HD), jnp.float32)
            for head in range(heads):
                total = jnp.sum(products[:, head * HD : (head + 1) * HD], axis=1, keepdims=True)
                scores = jnp.where(head_lane[: rows.shape[0]] == head, total, scores)
            return scores * factor

        own = by_head(new_kv[slot, 0:1, :].astype(jnp.float32))
        scores = []
        for half in range(2):
            place = 2 * lax.broadcasted_iota(jnp.int32, (steps, HD), 0) + half
            distance = (lens[slot] - place).astype(jnp.float32)
            found = by_head(cache[half, 0, slot].astype(jnp.float32)) - slope * distance
            scores.append(jnp.where(place < lens[slot], found, -jnp.inf))
        top = jnp.maximum(jnp.max(jnp.maximum(scores[0], scores[1]), axis=0, keepdims=True), own)
        raised = [jnp.exp(score - top) for score in scores]
        own_raised = jnp.exp(own - top)
        total = jnp.sum(raised[0] + raised[1], axis=0, keepdims=True) + own_raised
        weights = [(part / total).astype(jnp.bfloat16).astype(jnp.float32) for part in raised]
        own_weight = (own_raised / total).astype(jnp.bfloat16).astype(jnp.float32)
        for head in range(heads):
            lanes = slice(head * HD, (head + 1) * HD)
            mixed = jnp.zeros((steps, HD), jnp.float32)
            for half in range(2):
                values = cache[half, 1, slot, :, lanes].astype(jnp.float32)
                mixed += weights[half][:, head : head + 1] * values
            mixed = jnp.sum(mixed, axis=0, keepdims=True) + own_weight[:, head : head + 1] * own_value[:, lanes]
            out[slot : slot + 1, lanes] = mixed.astype(jnp.bfloat16)


def attend(lens, slopes, cache, query, new_kv, result):
    return pl.pallas_call(
        attend_kernel,
        out_shape=jax.ShapeDtypeStruct(query.shape, jnp.bfloat16),
        in_specs=[SMEM, SMEM, VMEM, VMEM, VMEM, VMEM],
        out_specs=VMEM,
        compiler_params=pltpu.CompilerParams(vmem_limit_bytes=KERNEL_VMEM),
        cost_estimate=pl.CostEstimate(flops=8 * cache.size, bytes_accessed=2 * cache.size, transcendentals=cache.size // HD),
        name="attend",
    )(lens, slopes, cache, query, new_kv, result)


def per_device(stored_rows, kv_weight, lengths, new_place, query, new_kv):
    groups = lax.axis_size("dp")
    planes = lax.axis_size("tensor")
    group_index = lax.axis_index("dp")
    tensor_index = lax.axis_index("tensor")
    core = jnp.bitwise_and(group_index, 1)
    half = jnp.bitwise_and(jnp.right_shift(group_index, 3) + jnp.right_shift(group_index, 1), 1)
    requests = lengths.shape[0]
    columns = kv_weight.shape[2]
    heads_here = columns // HD

    sent = split_rows(stored_rows, groups)
    parts = lax.all_to_all(sent, "dp", split_axis=0, concat_axis=0, tiled=True)
    w_own = kv_weight.transpose(1, 0, 2)
    w_next = lax.ppermute(w_own, "dp", [(i, partner(i)) for i in range(groups)])

    slots = jnp.arange(requests, dtype=jnp.int32)
    at_slot = new_place[None, :] == slots[:, None]
    source = jnp.sum(jnp.where(at_slot, slots[None, :], 0), axis=1)
    slot_len = jnp.sum(jnp.where(at_slot, lengths[None, :], 0), axis=1)
    steps = LMAX // 2
    step = jnp.arange(steps, dtype=jnp.int32)
    plane = (source % 2)[:, None] * steps + step[None, :]
    row = plane * groups + (source // 2)[:, None]
    live = (2 * step + half)[None, :] < slot_len[:, None]
    row = jnp.where(live, row, -1).reshape(-1)
    route = (row[:, None] == jnp.arange(planes * groups, dtype=jnp.int32)[None, :]).astype(jnp.bfloat16)

    every = lax.all_gather(join_rows(parts, row), "tensor", axis=0, tiled=True)
    where = core.reshape(1).astype(jnp.int32)
    away = product(False, where, every, w_own, w_next)
    received = lax.ppermute(away, "dp", [(i, i ^ 1) for i in range(groups)])
    partial = add(product(True, where, every, w_own, w_next), received, route)

    arrived = lax.all_to_all(
        partial.reshape(groups, REQ_DEV * steps, columns), "dp", split_axis=0, concat_axis=0, tiled=True
    )
    arrived = arrived.reshape(2, 2, 2, 2, CORES, REQ_DEV, steps, columns)
    summed = jnp.sum(arrived, axis=(0, 2), dtype=jnp.float32)
    summed = jnp.stack([summed[0, 0] + summed[1, 1], summed[0, 1] + summed[1, 0]]).astype(jnp.bfloat16)
    kv_cache = summed.transpose(2, 3, 0, 1, 4).reshape(REQ_DEV, LMAX, 2, columns)
    here_len = lax.dynamic_slice_in_dim(slot_len, group_index * REQ_DEV, REQ_DEV)
    slopes = lax.dynamic_slice_in_dim(alibi_slopes(HEADS), tensor_index * heads_here, heads_here)
    return (kv_cache, attend(here_len, slopes, summed, query, new_kv, kv_cache))


def solution(mesh):
    placed = (
        P(("dp", "tensor"), None),
        P("dp", None, "tensor"),
        P(),
        P(),
        P("dp", "tensor"),
        P("dp", None, "tensor"),
    )
    return jax.shard_map(
        per_device,
        mesh=mesh,
        in_specs=placed,
        out_specs=(P("dp", None, None, "tensor"), P("dp", "tensor")),
        check_vma=False,
    )
```

```python
import functools
import math

import jax
import jax.numpy as jnp
from jax import lax
from jax.experimental import pallas as pl
from jax.experimental.pallas import tpu as pltpu
from jax.sharding import PartitionSpec as P

HEADS = 112
HD = 128
REQ_DEV = 2
LMAX = 16


def alibi_slopes(count):
    closest = 2 ** int(math.floor(math.log2(count)))
    counted = jnp.arange(count, dtype=jnp.float32)
    leading = jnp.exp2(-8.0 * (counted + 1.0) / closest)
    trailing = jnp.exp2(-4.0 * (2.0 * (counted - closest) + 1.0) / closest)
    return jnp.where(counted < closest, leading, trailing)


VMEM = pl.BlockSpec(memory_space=pltpu.VMEM)
SMEM = pl.BlockSpec(memory_space=pltpu.SMEM)
ANYWHERE = pl.BlockSpec(memory_space=pl.ANY)
HBM = pl.BlockSpec(memory_space=pltpu.HBM)
KERNEL_VMEM = 24 * 1024 * 1024
SIDE = 4
CORES = 2


def partner(index):
    return index ^ (2 * SIDE if index % CORES == 0 else CORES)


def parity(index):
    return (index // (CORES * SIDE) + index // CORES) % 2


def split_rows_kernel(rows, weights, sent, same):
    del weights, same
    groups, share, block = sent.shape
    for to in range(groups):
        row = parity(to)
        for part, at in enumerate((to, partner(to))):
            sent[to, part : part + 1, :] = rows[row : row + 1, at * block : (at + 1) * block]


def split_rows(rows, weights, groups):
    block = rows.shape[1] // groups
    return pl.pallas_call(
        split_rows_kernel,
        out_shape=[
            jax.ShapeDtypeStruct((groups, 2, block), jnp.bfloat16),
            jax.ShapeDtypeStruct(weights.shape, weights.dtype),
        ],
        in_specs=[VMEM, ANYWHERE],
        out_specs=[VMEM, ANYWHERE],
        input_output_aliases={1: 1},
        compiler_params=pltpu.CompilerParams(vmem_limit_bytes=KERNEL_VMEM),
        name="split_rows",
    )(rows, weights)


def join_rows_kernel(parts, row, rows):
    del row
    block = parts.shape[2]
    rows[:, :block] = parts[:, 0, :]
    rows[:, block:] = parts[:, 1, :]


def join_rows(parts, row):
    groups, share, block = parts.shape
    return pl.pallas_call(
        join_rows_kernel,
        out_shape=jax.ShapeDtypeStruct((groups, share * block), jnp.bfloat16),
        in_specs=[VMEM, HBM],
        out_specs=VMEM,
        compiler_params=pltpu.CompilerParams(vmem_limit_bytes=KERNEL_VMEM),
        cost_estimate=pl.CostEstimate(flops=34500000000, bytes_accessed=0, transcendentals=0),
        name="join_rows",
    )(parts, row)


def fetch(moves, sems):
    copies = [pltpu.make_async_copy(source, to, sems.at[at]) for at, (source, to) in enumerate(moves)]
    for copy in copies:
        copy.start()
    return copies


def finish(copies):
    for copy in copies:
        copy.wait()


def product_kernel(home, where, x, w_own, w_next, out, held, sems):
    column = where[0] if home else 1 - where[0]
    block = w_own.shape[1]
    copies = fetch([(w_next.at[column], held)], sems)
    total = jnp.dot(x[:, :block], w_own[column], preferred_element_type=jnp.float32)
    finish(copies)
    total += jnp.dot(x[:, block:], held[...], preferred_element_type=jnp.float32)
    out[...] = total.astype(jnp.bfloat16)


def product(home, where, x, w_own, w_next):
    rows, depth = x.shape
    columns = w_own.shape[2]
    return pl.pallas_call(
        functools.partial(product_kernel, home),
        out_shape=jax.ShapeDtypeStruct((rows, columns), jnp.bfloat16),
        in_specs=[SMEM, VMEM, VMEM, ANYWHERE],
        out_specs=VMEM,
        scratch_shapes=[pltpu.VMEM(w_next.shape[1:], jnp.bfloat16), pltpu.SemaphoreType.DMA((1,))],
        compiler_params=pltpu.CompilerParams(vmem_limit_bytes=KERNEL_VMEM),
        cost_estimate=pl.CostEstimate(
            flops=2 * rows * depth * columns,
            bytes_accessed=2 * (rows * depth + depth * columns + rows * columns),
            transcendentals=0,
        ),
        name="home" if home else "away",
    )(where, x, w_own, w_next)


def add_kernel(one, other, route, total):
    both = (one[...].astype(jnp.float32) + other[...].astype(jnp.float32)).astype(jnp.bfloat16)
    total[...] = jnp.dot(route[...], both, preferred_element_type=jnp.float32).astype(jnp.bfloat16)


def add(one, other, route):
    return pl.pallas_call(
        add_kernel,
        out_shape=jax.ShapeDtypeStruct(one.shape, jnp.bfloat16),
        in_specs=[VMEM, VMEM, VMEM],
        out_specs=VMEM,
        compiler_params=pltpu.CompilerParams(vmem_limit_bytes=KERNEL_VMEM),
        cost_estimate=pl.CostEstimate(
            flops=2 * one.size * route.shape[0], bytes_accessed=6 * one.size + 2 * route.size, transcendentals=0
        ),
        name="add",
    )(one, other, route)


def attend_kernel(lens, slopes, cache, query, new_kv, result, out):
    del result
    slots, columns = query.shape
    heads = columns // HD
    steps = cache.shape[3]
    factor = 1.0 / math.sqrt(HD)
    head_lane = lax.broadcasted_iota(jnp.int32, (steps, HD), 1)
    slope = jnp.zeros((steps, HD), jnp.float32)
    for head in range(heads):
        slope = jnp.where(head_lane == head, slopes[head], slope)
    for slot in range(slots):
        asked = query[slot : slot + 1, :].astype(jnp.float32)
        own_value = new_kv[slot, 1:2, :].astype(jnp.float32)

        def by_head(rows):
            products = rows * asked
            scores = jnp.zeros((rows.shape[0], HD), jnp.float32)
            for head in range(heads):
                total = jnp.sum(products[:, head * HD : (head + 1) * HD], axis=1, keepdims=True)
                scores = jnp.where(head_lane[: rows.shape[0]] == head, total, scores)
            return scores * factor

        own = by_head(new_kv[slot, 0:1, :].astype(jnp.float32))
        scores = []
        for half in range(2):
            place = 2 * lax.broadcasted_iota(jnp.int32, (steps, HD), 0) + half
            distance = (lens[slot] - place).astype(jnp.float32)
            found = by_head(cache[half, 0, slot].astype(jnp.float32)) - slope * distance
            scores.append(jnp.where(place < lens[slot], found, -jnp.inf))
        top = jnp.maximum(jnp.max(jnp.maximum(scores[0], scores[1]), axis=0, keepdims=True), own)
        raised = [jnp.exp(score - top) for score in scores]
        own_raised = jnp.exp(own - top)
        total = jnp.sum(raised[0] + raised[1], axis=0, keepdims=True) + own_raised
        weights = [(part / total).astype(jnp.bfloat16).astype(jnp.float32) for part in raised]
        own_weight = (own_raised / total).astype(jnp.bfloat16).astype(jnp.float32)
        for head in range(heads):
            lanes = slice(head * HD, (head + 1) * HD)
            mixed = jnp.zeros((steps, HD), jnp.float32)
            for half in range(2):
                values = cache[half, 1, slot, :, lanes].astype(jnp.float32)
                mixed += weights[half][:, head : head + 1] * values
            mixed = jnp.sum(mixed, axis=0, keepdims=True) + own_weight[:, head : head + 1] * own_value[:, lanes]
            out[slot : slot + 1, lanes] = mixed.astype(jnp.bfloat16)


def attend(lens, slopes, cache, query, new_kv, result):
    return pl.pallas_call(
        attend_kernel,
        out_shape=jax.ShapeDtypeStruct(query.shape, jnp.bfloat16),
        in_specs=[SMEM, SMEM, VMEM, VMEM, VMEM, VMEM],
        out_specs=VMEM,
        compiler_params=pltpu.CompilerParams(vmem_limit_bytes=KERNEL_VMEM),
        cost_estimate=pl.CostEstimate(flops=8 * cache.size, bytes_accessed=2 * cache.size, transcendentals=cache.size // HD),
        name="attend",
    )(lens, slopes, cache, query, new_kv, result)


def per_device(stored_rows, kv_weight, lengths, new_place, query, new_kv):
    groups = lax.axis_size("dp")
    planes = lax.axis_size("tensor")
    group_index = lax.axis_index("dp")
    tensor_index = lax.axis_index("tensor")
    core = jnp.bitwise_and(group_index, 1)
    half = jnp.bitwise_and(jnp.right_shift(group_index, 3) + jnp.right_shift(group_index, 1), 1)
    requests = lengths.shape[0]
    columns = kv_weight.shape[2]
    heads_here = columns // HD

    w_own = kv_weight.transpose(1, 0, 2)
    sent, w_own = split_rows(stored_rows, w_own, groups)
    parts = lax.all_to_all(sent, "dp", split_axis=0, concat_axis=0, tiled=True)
    w_next = lax.ppermute(w_own, "dp", [(i, partner(i)) for i in range(groups)])

    slots = jnp.arange(requests, dtype=jnp.int32)
    at_slot = new_place[None, :] == slots[:, None]
    source = jnp.sum(jnp.where(at_slot, slots[None, :], 0), axis=1)
    slot_len = jnp.sum(jnp.where(at_slot, lengths[None, :], 0), axis=1)
    steps = LMAX // 2
    step = jnp.arange(steps, dtype=jnp.int32)
    plane = (source % 2)[:, None] * steps + step[None, :]
    row = plane * groups + (source // 2)[:, None]
    live = (2 * step + half)[None, :] < slot_len[:, None]
    row = jnp.where(live, row, -1).reshape(-1)
    route = (row[:, None] == jnp.arange(planes * groups, dtype=jnp.int32)[None, :]).astype(jnp.bfloat16)

    every = lax.all_gather(join_rows(parts, row), "tensor", axis=0, tiled=True)
    where = core.reshape(1).astype(jnp.int32)
    away = product(False, where, every, w_own, w_next)
    received = lax.ppermute(away, "dp", [(i, i ^ 1) for i in range(groups)])
    partial = add(product(True, where, every, w_own, w_next), received, route)

    arrived = lax.all_to_all(
        partial.reshape(groups, REQ_DEV * steps, columns), "dp", split_axis=0, concat_axis=0, tiled=True
    )
    arrived = arrived.reshape(2, 2, 2, 2, CORES, REQ_DEV, steps, columns)
    summed = jnp.sum(arrived, axis=(0, 2), dtype=jnp.float32)
    summed = jnp.stack([summed[0, 0] + summed[1, 1], summed[0, 1] + summed[1, 0]]).astype(jnp.bfloat16)
    kv_cache = summed.transpose(2, 3, 0, 1, 4).reshape(REQ_DEV, LMAX, 2, columns)
    here_len = lax.dynamic_slice_in_dim(slot_len, group_index * REQ_DEV, REQ_DEV)
    slopes = lax.dynamic_slice_in_dim(alibi_slopes(HEADS), tensor_index * heads_here, heads_here)
    return (kv_cache, attend(here_len, slopes, summed, query, new_kv, kv_cache))


def solution(mesh):
    placed = (
        P(("dp", "tensor"), None),
        P("dp", None, "tensor"),
        P(),
        P(),
        P("dp", "tensor"),
        P("dp", None, "tensor"),
    )
    return jax.shard_map(
        per_device,
        mesh=mesh,
        in_specs=placed,
        out_specs=(P("dp", None, None, "tensor"), P("dp", "tensor")),
        check_vma=False,
    )
```

```python
import functools
import math

import jax
import jax.numpy as jnp
from jax import lax
from jax.experimental import pallas as pl
from jax.experimental.pallas import tpu as pltpu
from jax.sharding import PartitionSpec as P

HEADS = 112
HD = 128
REQ_DEV = 2
LMAX = 16


def alibi_slopes(count):
    closest = 2 ** int(math.floor(math.log2(count)))
    counted = jnp.arange(count, dtype=jnp.float32)
    leading = jnp.exp2(-8.0 * (counted + 1.0) / closest)
    trailing = jnp.exp2(-4.0 * (2.0 * (counted - closest) + 1.0) / closest)
    return jnp.where(counted < closest, leading, trailing)


VMEM = pl.BlockSpec(memory_space=pltpu.VMEM)
SMEM = pl.BlockSpec(memory_space=pltpu.SMEM)
ANYWHERE = pl.BlockSpec(memory_space=pl.ANY)
HBM = pl.BlockSpec(memory_space=pltpu.HBM)
KERNEL_VMEM = 24 * 1024 * 1024
SIDE = 4
CORES = 2
TILE = 512


def partner(index):
    return index ^ (2 * SIDE if index % CORES == 0 else CORES)


def parity(index):
    return (index // (CORES * SIDE) + index // CORES) % 2


def split_rows_kernel(rows, weights, sent, same):
    del weights, same
    groups, share, block = sent.shape
    for to in range(groups):
        row = parity(to)
        for part, at in enumerate((to, partner(to))):
            sent[to, part : part + 1, :] = rows[row : row + 1, at * block : (at + 1) * block]


def split_rows(rows, weights, groups):
    block = rows.shape[1] // groups
    return pl.pallas_call(
        split_rows_kernel,
        out_shape=[
            jax.ShapeDtypeStruct((groups, 2, block), jnp.bfloat16),
            jax.ShapeDtypeStruct(weights.shape, weights.dtype),
        ],
        in_specs=[VMEM, ANYWHERE],
        out_specs=[VMEM, ANYWHERE],
        input_output_aliases={1: 1},
        compiler_params=pltpu.CompilerParams(vmem_limit_bytes=KERNEL_VMEM),
        name="split_rows",
    )(rows, weights)


def join_rows_kernel(parts, row, rows):
    del row
    block = parts.shape[2]
    rows[:, :block] = parts[:, 0, :]
    rows[:, block:] = parts[:, 1, :]


def join_rows(parts, row):
    groups, share, block = parts.shape
    return pl.pallas_call(
        join_rows_kernel,
        out_shape=jax.ShapeDtypeStruct((groups, share * block), jnp.bfloat16),
        in_specs=[VMEM, HBM],
        out_specs=VMEM,
        compiler_params=pltpu.CompilerParams(vmem_limit_bytes=KERNEL_VMEM),
        cost_estimate=pl.CostEstimate(flops=34500000000, bytes_accessed=0, transcendentals=0),
        name="join_rows",
    )(parts, row)


def fetch(moves, sems):
    copies = [pltpu.make_async_copy(source, to, sems.at[at]) for at, (source, to) in enumerate(moves)]
    for copy in copies:
        copy.start()
    return copies


def finish(copies):
    for copy in copies:
        copy.wait()


def product_kernel(home, where, x, w_own, w_next, out):
    column = where[0] if home else 1 - where[0]
    block = w_own.shape[1]
    total = jnp.dot(x[:, :block], w_own[column], preferred_element_type=jnp.float32)
    total += jnp.dot(x[:, block:], w_next[column], preferred_element_type=jnp.float32)
    out[...] = total.astype(jnp.bfloat16)


def product(home, where, x, w_own, w_next):
    rows, depth = x.shape
    columns = w_own.shape[2]
    return pl.pallas_call(
        functools.partial(product_kernel, home),
        out_shape=jax.ShapeDtypeStruct((rows, columns), jnp.bfloat16),
        in_specs=[SMEM, VMEM, VMEM, VMEM],
        out_specs=VMEM,
        compiler_params=pltpu.CompilerParams(vmem_limit_bytes=KERNEL_VMEM),
        cost_estimate=pl.CostEstimate(
            flops=2 * rows * depth * columns,
            bytes_accessed=2 * (rows * depth + depth * columns + rows * columns),
            transcendentals=0,
        ),
        name="home" if home else "away",
    )(where, x, w_own, w_next)


def add_kernel(one, other, route, total, made, sems):
    columns = total.shape[1]
    copies = []
    for at, (start, stop) in enumerate(((0, TILE), (TILE, columns))):
        part = pl.ds(start, stop - start)
        both = (one[:, part].astype(jnp.float32) + other[:, part].astype(jnp.float32)).astype(jnp.bfloat16)
        made[:, part] = jnp.dot(route[...], both, preferred_element_type=jnp.float32).astype(jnp.bfloat16)
        copies += fetch([(made.at[:, part], total.at[:, part])], sems.at[pl.ds(at, 1)])
    finish(copies)


def add(one, other, route):
    return pl.pallas_call(
        add_kernel,
        out_shape=jax.ShapeDtypeStruct(one.shape, jnp.bfloat16),
        in_specs=[VMEM, VMEM, VMEM],
        out_specs=ANYWHERE,
        scratch_shapes=[pltpu.VMEM(one.shape, jnp.bfloat16), pltpu.SemaphoreType.DMA((2,))],
        compiler_params=pltpu.CompilerParams(vmem_limit_bytes=KERNEL_VMEM),
        cost_estimate=pl.CostEstimate(
            flops=2 * one.size * route.shape[0], bytes_accessed=6 * one.size + 2 * route.size, transcendentals=0
        ),
        name="add",
    )(one, other, route)


def attend_kernel(lens, slopes, cache, query, new_kv, result, out):
    del result
    slots, columns = query.shape
    heads = columns // HD
    steps = cache.shape[3]
    factor = 1.0 / math.sqrt(HD)
    head_lane = lax.broadcasted_iota(jnp.int32, (steps, HD), 1)
    slope = jnp.zeros((steps, HD), jnp.float32)
    for head in range(heads):
        slope = jnp.where(head_lane == head, slopes[head], slope)
    for slot in range(slots):
        asked = query[slot : slot + 1, :].astype(jnp.float32)
        own_value = new_kv[slot, 1:2, :].astype(jnp.float32)

        def by_head(rows):
            products = rows * asked
            scores = jnp.zeros((rows.shape[0], HD), jnp.float32)
            for head in range(heads):
                total = jnp.sum(products[:, head * HD : (head + 1) * HD], axis=1, keepdims=True)
                scores = jnp.where(head_lane[: rows.shape[0]] == head, total, scores)
            return scores * factor

        own = by_head(new_kv[slot, 0:1, :].astype(jnp.float32))
        scores = []
        for half in range(2):
            place = 2 * lax.broadcasted_iota(jnp.int32, (steps, HD), 0) + half
            distance = (lens[slot] - place).astype(jnp.float32)
            found = by_head(cache[half, 0, slot].astype(jnp.float32)) - slope * distance
            scores.append(jnp.where(place < lens[slot], found, -jnp.inf))
        top = jnp.maximum(jnp.max(jnp.maximum(scores[0], scores[1]), axis=0, keepdims=True), own)
        raised = [jnp.exp(score - top) for score in scores]
        own_raised = jnp.exp(own - top)
        total = jnp.sum(raised[0] + raised[1], axis=0, keepdims=True) + own_raised
        weights = [(part / total).astype(jnp.bfloat16).astype(jnp.float32) for part in raised]
        own_weight = (own_raised / total).astype(jnp.bfloat16).astype(jnp.float32)
        for head in range(heads):
            lanes = slice(head * HD, (head + 1) * HD)
            mixed = jnp.zeros((steps, HD), jnp.float32)
            for half in range(2):
                values = cache[half, 1, slot, :, lanes].astype(jnp.float32)
                mixed += weights[half][:, head : head + 1] * values
            mixed = jnp.sum(mixed, axis=0, keepdims=True) + own_weight[:, head : head + 1] * own_value[:, lanes]
            out[slot : slot + 1, lanes] = mixed.astype(jnp.bfloat16)


def attend(lens, slopes, cache, query, new_kv, result):
    return pl.pallas_call(
        attend_kernel,
        out_shape=jax.ShapeDtypeStruct(query.shape, jnp.bfloat16),
        in_specs=[SMEM, SMEM, VMEM, VMEM, VMEM, VMEM],
        out_specs=VMEM,
        compiler_params=pltpu.CompilerParams(vmem_limit_bytes=KERNEL_VMEM),
        cost_estimate=pl.CostEstimate(flops=8 * cache.size, bytes_accessed=2 * cache.size, transcendentals=cache.size // HD),
        name="attend",
    )(lens, slopes, cache, query, new_kv, result)


def per_device(stored_rows, kv_weight, lengths, new_place, query, new_kv):
    groups = lax.axis_size("dp")
    planes = lax.axis_size("tensor")
    group_index = lax.axis_index("dp")
    tensor_index = lax.axis_index("tensor")
    core = jnp.bitwise_and(group_index, 1)
    half = jnp.bitwise_and(jnp.right_shift(group_index, 3) + jnp.right_shift(group_index, 1), 1)
    requests = lengths.shape[0]
    columns = kv_weight.shape[2]
    heads_here = columns // HD

    w_own = kv_weight.transpose(1, 0, 2)
    sent, w_own = split_rows(stored_rows, w_own, groups)
    parts = lax.all_to_all(sent, "dp", split_axis=0, concat_axis=0, tiled=True)
    w_next = lax.ppermute(w_own, "dp", [(i, partner(i)) for i in range(groups)])

    slots = jnp.arange(requests, dtype=jnp.int32)
    at_slot = new_place[None, :] == slots[:, None]
    source = jnp.sum(jnp.where(at_slot, slots[None, :], 0), axis=1)
    slot_len = jnp.sum(jnp.where(at_slot, lengths[None, :], 0), axis=1)
    steps = LMAX // 2
    step = jnp.arange(steps, dtype=jnp.int32)
    plane = (source % 2)[:, None] * steps + step[None, :]
    row = plane * groups + (source // 2)[:, None]
    live = (2 * step + half)[None, :] < slot_len[:, None]
    row = jnp.where(live, row, -1).reshape(-1)
    route = (row[:, None] == jnp.arange(planes * groups, dtype=jnp.int32)[None, :]).astype(jnp.bfloat16)

    every = lax.all_gather(join_rows(parts, row), "tensor", axis=0, tiled=True)
    where = core.reshape(1).astype(jnp.int32)
    away = product(False, where, every, w_own, w_next)
    received = lax.ppermute(away, "dp", [(i, i ^ 1) for i in range(groups)])
    partial = add(product(True, where, every, w_own, w_next), received, route)

    arrived = lax.all_to_all(
        partial.reshape(groups, REQ_DEV * steps, columns), "dp", split_axis=0, concat_axis=0, tiled=True
    )
    arrived = arrived.reshape(2, 2, 2, 2, CORES, REQ_DEV, steps, columns)
    summed = jnp.sum(arrived, axis=(0, 2), dtype=jnp.float32)
    summed = jnp.stack([summed[0, 0] + summed[1, 1], summed[0, 1] + summed[1, 0]]).astype(jnp.bfloat16)
    kv_cache = summed.transpose(2, 3, 0, 1, 4).reshape(REQ_DEV, LMAX, 2, columns)
    here_len = lax.dynamic_slice_in_dim(slot_len, group_index * REQ_DEV, REQ_DEV)
    slopes = lax.dynamic_slice_in_dim(alibi_slopes(HEADS), tensor_index * heads_here, heads_here)
    return (kv_cache, attend(here_len, slopes, summed, query, new_kv, kv_cache))


def solution(mesh):
    placed = (
        P(("dp", "tensor"), None),
        P("dp", None, "tensor"),
        P(),
        P(),
        P("dp", "tensor"),
        P("dp", None, "tensor"),
    )
    return jax.shard_map(
        per_device,
        mesh=mesh,
        in_specs=placed,
        out_specs=(P("dp", None, None, "tensor"), P("dp", "tensor")),
        check_vma=False,
    )
```

```python
import functools
import math

import jax
import jax.numpy as jnp
from jax import lax
from jax.experimental import pallas as pl
from jax.experimental.pallas import tpu as pltpu
from jax.sharding import PartitionSpec as P

HEADS = 112
HD = 128
REQ_DEV = 2
LMAX = 16


def alibi_slopes(count):
    closest = 2 ** int(math.floor(math.log2(count)))
    counted = jnp.arange(count, dtype=jnp.float32)
    leading = jnp.exp2(-8.0 * (counted + 1.0) / closest)
    trailing = jnp.exp2(-4.0 * (2.0 * (counted - closest) + 1.0) / closest)
    return jnp.where(counted < closest, leading, trailing)


VMEM = pl.BlockSpec(memory_space=pltpu.VMEM)
SMEM = pl.BlockSpec(memory_space=pltpu.SMEM)
ANYWHERE = pl.BlockSpec(memory_space=pl.ANY)
HBM = pl.BlockSpec(memory_space=pltpu.HBM)
KERNEL_VMEM = 24 * 1024 * 1024
SIDE = 4
CORES = 2
TILE = 512


def partner(index):
    return index ^ (2 * SIDE if index % CORES == 0 else CORES)


def parity(index):
    return (index // (CORES * SIDE) + index // CORES) % 2


def split_rows_kernel(rows, weights, sent, same):
    del weights, same
    groups, share, block = sent.shape
    for to in range(groups):
        row = parity(to)
        for part, at in enumerate((to, partner(to))):
            sent[to, part : part + 1, :] = rows[row : row + 1, at * block : (at + 1) * block]


def split_rows(rows, weights, groups):
    block = rows.shape[1] // groups
    return pl.pallas_call(
        split_rows_kernel,
        out_shape=[
            jax.ShapeDtypeStruct((groups, 2, block), jnp.bfloat16),
            jax.ShapeDtypeStruct(weights.shape, weights.dtype),
        ],
        in_specs=[VMEM, ANYWHERE],
        out_specs=[VMEM, ANYWHERE],
        input_output_aliases={1: 1},
        compiler_params=pltpu.CompilerParams(vmem_limit_bytes=KERNEL_VMEM),
        name="split_rows",
    )(rows, weights)


def join_rows_kernel(parts, row, rows):
    del row
    block = parts.shape[2]
    rows[:, :block] = parts[:, 0, :]
    rows[:, block:] = parts[:, 1, :]


def join_rows(parts, row):
    groups, share, block = parts.shape
    return pl.pallas_call(
        join_rows_kernel,
        out_shape=jax.ShapeDtypeStruct((groups, share * block), jnp.bfloat16),
        in_specs=[VMEM, HBM],
        out_specs=VMEM,
        compiler_params=pltpu.CompilerParams(vmem_limit_bytes=KERNEL_VMEM),
        cost_estimate=pl.CostEstimate(flops=34500000000, bytes_accessed=0, transcendentals=0),
        name="join_rows",
    )(parts, row)


def fetch(moves, sems):
    copies = [pltpu.make_async_copy(source, to, sems.at[at]) for at, (source, to) in enumerate(moves)]
    for copy in copies:
        copy.start()
    return copies


def finish(copies):
    for copy in copies:
        copy.wait()


def product_kernel(home, where, x, w_own, w_next, out):
    column = where[0] if home else 1 - where[0]
    block = w_own.shape[1]
    total = jnp.dot(x[:, :block], w_own[column], preferred_element_type=jnp.float32)
    total += jnp.dot(x[:, block:], w_next[column], preferred_element_type=jnp.float32)
    out[...] = total.astype(jnp.bfloat16)


def product(home, where, x, w_own, w_next):
    rows, depth = x.shape
    columns = w_own.shape[2]
    return pl.pallas_call(
        functools.partial(product_kernel, home),
        out_shape=jax.ShapeDtypeStruct((rows, columns), jnp.bfloat16),
        in_specs=[SMEM, VMEM, VMEM, VMEM],
        out_specs=VMEM,
        compiler_params=pltpu.CompilerParams(vmem_limit_bytes=KERNEL_VMEM),
        cost_estimate=pl.CostEstimate(
            flops=2 * rows * depth * columns,
            bytes_accessed=2 * (rows * depth + depth * columns + rows * columns),
            transcendentals=0,
        ),
        name="home" if home else "away",
    )(where, x, w_own, w_next)


def add_kernel(one, other, route, total, made, sems):
    columns = total.shape[1]
    copies = []
    for at, (start, stop) in enumerate(((0, TILE), (TILE, columns))):
        part = pl.ds(start, stop - start)
        both = (one[:, part].astype(jnp.float32) + other[:, part].astype(jnp.float32)).astype(jnp.bfloat16)
        made[:, part] = jnp.dot(route[...], both, preferred_element_type=jnp.float32).astype(jnp.bfloat16)
        copies += fetch([(made.at[:, part], total.at[:, part])], sems.at[pl.ds(at, 1)])
    finish(copies)


def add(one, other, route):
    return pl.pallas_call(
        add_kernel,
        out_shape=jax.ShapeDtypeStruct(one.shape, jnp.bfloat16),
        in_specs=[VMEM, VMEM, VMEM],
        out_specs=ANYWHERE,
        scratch_shapes=[pltpu.VMEM(one.shape, jnp.bfloat16), pltpu.SemaphoreType.DMA((2,))],
        compiler_params=pltpu.CompilerParams(vmem_limit_bytes=KERNEL_VMEM),
        cost_estimate=pl.CostEstimate(
            flops=2 * one.size * route.shape[0], bytes_accessed=6 * one.size + 2 * route.size, transcendentals=0
        ),
        name="add",
    )(one, other, route)


def attend_kernel(lens, slopes, cache, query, new_kv, result, out):
    del result
    slots, columns = query.shape
    heads = columns // HD
    steps = cache.shape[3]
    factor = 1.0 / math.sqrt(HD)
    head_lane = lax.broadcasted_iota(jnp.int32, (2 * steps, HD), 1)
    step = lax.broadcasted_iota(jnp.int32, (2 * steps, HD), 0)
    place = jnp.where(step < steps, 2 * step, 2 * (step - steps) + 1)
    for slot in range(slots):
        asked = query[slot : slot + 1, :].astype(jnp.float32)
        own_value = new_kv[slot, 1:2, :].astype(jnp.float32)

        def by_head(rows):
            products = rows * asked
            scores = jnp.zeros((rows.shape[0], HD), jnp.float32)
            for head in range(heads):
                total = jnp.sum(products[:, head * HD : (head + 1) * HD], axis=1, keepdims=True)
                scores = jnp.where(head_lane[: rows.shape[0]] == head, total, scores)
            return scores * factor

        own = by_head(new_kv[slot, 0:1, :].astype(jnp.float32))
        keys = jnp.concatenate([cache[half, 0, slot].astype(jnp.float32) for half in range(2)], axis=0)
        values = jnp.concatenate([cache[half, 1, slot].astype(jnp.float32) for half in range(2)], axis=0)
        scores = by_head(keys) - slopes[...] * (lens[slot] - place).astype(jnp.float32)
        scores = jnp.where(place < lens[slot], scores, -jnp.inf)
        top = jnp.maximum(jnp.max(scores, axis=0, keepdims=True), own)
        raised = jnp.exp(scores - top)
        own_raised = jnp.exp(own - top)
        total = jnp.sum(raised, axis=0, keepdims=True) + own_raised
        weights = (raised / total).astype(jnp.bfloat16).astype(jnp.float32)
        own_weight = (own_raised / total).astype(jnp.bfloat16).astype(jnp.float32)
        for head in range(heads):
            lanes = slice(head * HD, (head + 1) * HD)
            mixed = jnp.sum(weights[:, head : head + 1] * values[:, lanes], axis=0, keepdims=True)
            mixed += own_weight[:, head : head + 1] * own_value[:, lanes]
            out[slot : slot + 1, lanes] = mixed.astype(jnp.bfloat16)


def attend(lens, slopes, cache, query, new_kv, result):
    return pl.pallas_call(
        attend_kernel,
        out_shape=jax.ShapeDtypeStruct(query.shape, jnp.bfloat16),
        in_specs=[SMEM, VMEM, VMEM, VMEM, VMEM, VMEM],
        out_specs=VMEM,
        compiler_params=pltpu.CompilerParams(vmem_limit_bytes=KERNEL_VMEM),
        cost_estimate=pl.CostEstimate(flops=8 * cache.size, bytes_accessed=2 * cache.size, transcendentals=cache.size // HD),
        name="attend",
    )(lens, slopes, cache, query, new_kv, result)


def per_device(stored_rows, kv_weight, lengths, new_place, query, new_kv):
    groups = lax.axis_size("dp")
    planes = lax.axis_size("tensor")
    group_index = lax.axis_index("dp")
    tensor_index = lax.axis_index("tensor")
    core = jnp.bitwise_and(group_index, 1)
    half = jnp.bitwise_and(jnp.right_shift(group_index, 3) + jnp.right_shift(group_index, 1), 1)
    requests = lengths.shape[0]
    columns = kv_weight.shape[2]
    heads_here = columns // HD

    w_own = kv_weight.transpose(1, 0, 2)
    sent, w_own = split_rows(stored_rows, w_own, groups)
    parts = lax.all_to_all(sent, "dp", split_axis=0, concat_axis=0, tiled=True)
    w_next = lax.ppermute(w_own, "dp", [(i, partner(i)) for i in range(groups)])

    slots = jnp.arange(requests, dtype=jnp.int32)
    at_slot = new_place[None, :] == slots[:, None]
    source = jnp.sum(jnp.where(at_slot, slots[None, :], 0), axis=1)
    slot_len = jnp.sum(jnp.where(at_slot, lengths[None, :], 0), axis=1)
    steps = LMAX // 2
    step = jnp.arange(steps, dtype=jnp.int32)
    plane = (source % 2)[:, None] * steps + step[None, :]
    row = plane * groups + (source // 2)[:, None]
    live = (2 * step + half)[None, :] < slot_len[:, None]
    row = jnp.where(live, row, -1).reshape(-1)
    route = (row[:, None] == jnp.arange(planes * groups, dtype=jnp.int32)[None, :]).astype(jnp.bfloat16)

    every = lax.all_gather(join_rows(parts, row), "tensor", axis=0, tiled=True)
    where = core.reshape(1).astype(jnp.int32)
    away = product(False, where, every, w_own, w_next)
    received = lax.ppermute(away, "dp", [(i, i ^ 1) for i in range(groups)])
    partial = add(product(True, where, every, w_own, w_next), received, route)

    arrived = lax.all_to_all(
        partial.reshape(groups, REQ_DEV * steps, columns), "dp", split_axis=0, concat_axis=0, tiled=True
    )
    arrived = arrived.reshape(2, 2, 2, 2, CORES, REQ_DEV, steps, columns)
    summed = jnp.sum(arrived, axis=(0, 2), dtype=jnp.float32)
    summed = jnp.stack([summed[0, 0] + summed[1, 1], summed[0, 1] + summed[1, 0]]).astype(jnp.bfloat16)
    kv_cache = summed.transpose(2, 3, 0, 1, 4).reshape(REQ_DEV, LMAX, 2, columns)
    here_len = lax.dynamic_slice_in_dim(slot_len, group_index * REQ_DEV, REQ_DEV)
    slopes = lax.dynamic_slice_in_dim(alibi_slopes(HEADS), tensor_index * heads_here, heads_here)
    return (kv_cache, attend(here_len, jnp.pad(slopes, (0, HD - heads_here)).reshape(1, HD), summed, query, new_kv, kv_cache))


def solution(mesh):
    placed = (
        P(("dp", "tensor"), None),
        P("dp", None, "tensor"),
        P(),
        P(),
        P("dp", "tensor"),
        P("dp", None, "tensor"),
    )
    return jax.shard_map(
        per_device,
        mesh=mesh,
        in_specs=placed,
        out_specs=(P("dp", None, None, "tensor"), P("dp", "tensor")),
        check_vma=False,
    )
```

```python
import functools
import math

import jax
import jax.numpy as jnp
from jax import lax
from jax.experimental import pallas as pl
from jax.experimental.pallas import tpu as pltpu
from jax.sharding import PartitionSpec as P

HEADS = 112
HD = 128
REQ_DEV = 2
LMAX = 16


def alibi_slopes(count):
    closest = 2 ** int(math.floor(math.log2(count)))
    counted = jnp.arange(count, dtype=jnp.float32)
    leading = jnp.exp2(-8.0 * (counted + 1.0) / closest)
    trailing = jnp.exp2(-4.0 * (2.0 * (counted - closest) + 1.0) / closest)
    return jnp.where(counted < closest, leading, trailing)


VMEM = pl.BlockSpec(memory_space=pltpu.VMEM)
SMEM = pl.BlockSpec(memory_space=pltpu.SMEM)
ANYWHERE = pl.BlockSpec(memory_space=pl.ANY)
HBM = pl.BlockSpec(memory_space=pltpu.HBM)
KERNEL_VMEM = 24 * 1024 * 1024
SIDE = 4
CORES = 2
TILE = 512


def partner(index):
    return index ^ (2 * SIDE if index % CORES == 0 else CORES)


def parity(index):
    return (index // (CORES * SIDE) + index // CORES) % 2


def split_rows_kernel(rows, weights, sent, same):
    del weights, same
    groups, share, block = sent.shape
    for to in range(groups):
        row = parity(to)
        parts = [rows[row : row + 1, at * block : (at + 1) * block] for at in (to, partner(to))]
        sent[to] = jnp.concatenate(parts, axis=0)


def split_rows(rows, weights, groups):
    block = rows.shape[1] // groups
    return pl.pallas_call(
        split_rows_kernel,
        out_shape=[
            jax.ShapeDtypeStruct((groups, 2, block), jnp.bfloat16),
            jax.ShapeDtypeStruct(weights.shape, weights.dtype),
        ],
        in_specs=[VMEM, ANYWHERE],
        out_specs=[VMEM, ANYWHERE],
        input_output_aliases={1: 1},
        compiler_params=pltpu.CompilerParams(vmem_limit_bytes=KERNEL_VMEM),
        name="split_rows",
    )(rows, weights)


def join_rows_kernel(parts, row, rows):
    del row
    block = parts.shape[2]
    rows[:, :block] = parts[:, 0, :]
    rows[:, block:] = parts[:, 1, :]


def join_rows(parts, row):
    groups, share, block = parts.shape
    return pl.pallas_call(
        join_rows_kernel,
        out_shape=jax.ShapeDtypeStruct((groups, share * block), jnp.bfloat16),
        in_specs=[VMEM, HBM],
        out_specs=VMEM,
        compiler_params=pltpu.CompilerParams(vmem_limit_bytes=KERNEL_VMEM),
        cost_estimate=pl.CostEstimate(flops=34500000000, bytes_accessed=0, transcendentals=0),
        name="join_rows",
    )(parts, row)


def fetch(moves, sems):
    copies = [pltpu.make_async_copy(source, to, sems.at[at]) for at, (source, to) in enumerate(moves)]
    for copy in copies:
        copy.start()
    return copies


def finish(copies):
    for copy in copies:
        copy.wait()


def product_kernel(home, where, x, w_own, w_next, out):
    column = where[0] if home else 1 - where[0]
    block = w_own.shape[1]
    total = jnp.dot(x[:, :block], w_own[column], preferred_element_type=jnp.float32)
    total += jnp.dot(x[:, block:], w_next[column], preferred_element_type=jnp.float32)
    out[...] = total.astype(jnp.bfloat16)


def product(home, where, x, w_own, w_next):
    rows, depth = x.shape
    columns = w_own.shape[2]
    return pl.pallas_call(
        functools.partial(product_kernel, home),
        out_shape=jax.ShapeDtypeStruct((rows, columns), jnp.bfloat16),
        in_specs=[SMEM, VMEM, VMEM, VMEM],
        out_specs=VMEM,
        compiler_params=pltpu.CompilerParams(vmem_limit_bytes=KERNEL_VMEM),
        cost_estimate=pl.CostEstimate(
            flops=2 * rows * depth * columns,
            bytes_accessed=2 * (rows * depth + depth * columns + rows * columns),
            transcendentals=0,
        ),
        name="home" if home else "away",
    )(where, x, w_own, w_next)


def add_kernel(one, other, route, total, made, sems):
    columns = total.shape[1]
    copies = []
    for at, (start, stop) in enumerate(((0, TILE), (TILE, columns))):
        part = pl.ds(start, stop - start)
        both = (one[:, part].astype(jnp.float32) + other[:, part].astype(jnp.float32)).astype(jnp.bfloat16)
        made[:, part] = jnp.dot(route[...], both, preferred_element_type=jnp.float32).astype(jnp.bfloat16)
        copies += fetch([(made.at[:, part], total.at[:, part])], sems.at[pl.ds(at, 1)])
    finish(copies)


def add(one, other, route):
    return pl.pallas_call(
        add_kernel,
        out_shape=jax.ShapeDtypeStruct(one.shape, jnp.bfloat16),
        in_specs=[VMEM, VMEM, VMEM],
        out_specs=ANYWHERE,
        scratch_shapes=[pltpu.VMEM(one.shape, jnp.bfloat16), pltpu.SemaphoreType.DMA((2,))],
        compiler_params=pltpu.CompilerParams(vmem_limit_bytes=KERNEL_VMEM),
        cost_estimate=pl.CostEstimate(
            flops=2 * one.size * route.shape[0], bytes_accessed=6 * one.size + 2 * route.size, transcendentals=0
        ),
        name="add",
    )(one, other, route)


def attend_kernel(lens, slopes, cache, query, new_kv, result, out):
    del result
    slots, columns = query.shape
    heads = columns // HD
    steps = cache.shape[3]
    factor = 1.0 / math.sqrt(HD)
    head_lane = lax.broadcasted_iota(jnp.int32, (2 * steps, HD), 1)
    step = lax.broadcasted_iota(jnp.int32, (2 * steps, HD), 0)
    place = jnp.where(step < steps, 2 * step, 2 * (step - steps) + 1)
    for slot in range(slots):
        asked = query[slot : slot + 1, :].astype(jnp.float32)
        own_value = new_kv[slot, 1:2, :].astype(jnp.float32)

        def by_head(rows):
            products = rows * asked
            scores = jnp.zeros((rows.shape[0], HD), jnp.float32)
            for head in range(heads):
                total = jnp.sum(products[:, head * HD : (head + 1) * HD], axis=1, keepdims=True)
                scores = jnp.where(head_lane[: rows.shape[0]] == head, total, scores)
            return scores * factor

        own = by_head(new_kv[slot, 0:1, :].astype(jnp.float32))
        keys = jnp.concatenate([cache[half, 0, slot].astype(jnp.float32) for half in range(2)], axis=0)
        values = jnp.concatenate([cache[half, 1, slot].astype(jnp.float32) for half in range(2)], axis=0)
        scores = by_head(keys) - slopes[...] * (lens[slot] - place).astype(jnp.float32)
        scores = jnp.where(place < lens[slot], scores, -jnp.inf)
        top = jnp.maximum(jnp.max(scores, axis=0, keepdims=True), own)
        raised = jnp.exp(scores - top)
        own_raised = jnp.exp(own - top)
        total = jnp.sum(raised, axis=0, keepdims=True) + own_raised
        weights = (raised / total).astype(jnp.bfloat16).astype(jnp.float32)
        own_weight = (own_raised / total).astype(jnp.bfloat16).astype(jnp.float32)
        for head in range(heads):
            lanes = slice(head * HD, (head + 1) * HD)
            mixed = jnp.sum(weights[:, head : head + 1] * values[:, lanes], axis=0, keepdims=True)
            mixed += own_weight[:, head : head + 1] * own_value[:, lanes]
            out[slot : slot + 1, lanes] = mixed.astype(jnp.bfloat16)


def attend(lens, slopes, cache, query, new_kv, result):
    return pl.pallas_call(
        attend_kernel,
        out_shape=jax.ShapeDtypeStruct(query.shape, jnp.bfloat16),
        in_specs=[SMEM, VMEM, VMEM, VMEM, VMEM, VMEM],
        out_specs=VMEM,
        compiler_params=pltpu.CompilerParams(vmem_limit_bytes=KERNEL_VMEM),
        cost_estimate=pl.CostEstimate(flops=8 * cache.size, bytes_accessed=2 * cache.size, transcendentals=cache.size // HD),
        name="attend",
    )(lens, slopes, cache, query, new_kv, result)


def per_device(stored_rows, kv_weight, lengths, new_place, query, new_kv):
    groups = lax.axis_size("dp")
    planes = lax.axis_size("tensor")
    group_index = lax.axis_index("dp")
    tensor_index = lax.axis_index("tensor")
    core = jnp.bitwise_and(group_index, 1)
    half = jnp.bitwise_and(jnp.right_shift(group_index, 3) + jnp.right_shift(group_index, 1), 1)
    requests = lengths.shape[0]
    columns = kv_weight.shape[2]
    heads_here = columns // HD

    w_own = kv_weight.transpose(1, 0, 2)
    sent, w_own = split_rows(stored_rows, w_own, groups)
    parts = lax.all_to_all(sent, "dp", split_axis=0, concat_axis=0, tiled=True)
    w_next = lax.ppermute(w_own, "dp", [(i, partner(i)) for i in range(groups)])

    slots = jnp.arange(requests, dtype=jnp.int32)
    at_slot = new_place[None, :] == slots[:, None]
    source = jnp.sum(jnp.where(at_slot, slots[None, :], 0), axis=1)
    slot_len = jnp.sum(jnp.where(at_slot, lengths[None, :], 0), axis=1)
    steps = LMAX // 2
    step = jnp.arange(steps, dtype=jnp.int32)
    plane = (source % 2)[:, None] * steps + step[None, :]
    row = plane * groups + (source // 2)[:, None]
    live = (2 * step + half)[None, :] < slot_len[:, None]
    row = jnp.where(live, row, -1).reshape(-1)
    route = (row[:, None] == jnp.arange(planes * groups, dtype=jnp.int32)[None, :]).astype(jnp.bfloat16)

    every = lax.all_gather(join_rows(parts, row), "tensor", axis=0, tiled=True)
    where = core.reshape(1).astype(jnp.int32)
    away = product(False, where, every, w_own, w_next)
    received = lax.ppermute(away, "dp", [(i, i ^ 1) for i in range(groups)])
    partial = add(product(True, where, every, w_own, w_next), received, route)

    arrived = lax.all_to_all(
        partial.reshape(groups, REQ_DEV * steps, columns), "dp", split_axis=0, concat_axis=0, tiled=True
    )
    arrived = arrived.reshape(2, 2, 2, 2, CORES, REQ_DEV, steps, columns)
    summed = jnp.sum(arrived, axis=(0, 2), dtype=jnp.float32)
    summed = jnp.stack([summed[0, 0] + summed[1, 1], summed[0, 1] + summed[1, 0]]).astype(jnp.bfloat16)
    kv_cache = summed.transpose(2, 3, 0, 1, 4).reshape(REQ_DEV, LMAX, 2, columns)
    here_len = lax.dynamic_slice_in_dim(slot_len, group_index * REQ_DEV, REQ_DEV)
    slopes = lax.dynamic_slice_in_dim(alibi_slopes(HEADS), tensor_index * heads_here, heads_here)
    return (kv_cache, attend(here_len, jnp.pad(slopes, (0, HD - heads_here)).reshape(1, HD), summed, query, new_kv, kv_cache))


def solution(mesh):
    placed = (
        P(("dp", "tensor"), None),
        P("dp", None, "tensor"),
        P(),
        P(),
        P("dp", "tensor"),
        P("dp", None, "tensor"),
    )
    return jax.shard_map(
        per_device,
        mesh=mesh,
        in_specs=placed,
        out_specs=(P("dp", None, None, "tensor"), P("dp", "tensor")),
        check_vma=False,
    )
```
